32 devices in a mesh: row: 2 (over y), col: 4 (over x, core), pair: 4 (over z).
Axes of the slice: x: 2, y: 2, z: 4, core: 2. Of those that a mesh axis runs over, the one named last changes fastest.
Arguments:
- amps: bfloat16 [512, 512, 512], P('pair', 'row', 'col'), may hold values from -6 to 6
- integrals: bfloat16 [4096, 512, 512], P('pair', 'row', 'col'), may hold values from -0.01171875 to 0.01171875
- mask_amps: int32 [8, 8], replicated, may hold values 0 or 1
- mask_ints: int32 [8, 8], replicated, may hold values 0 or 1
Outputs:
- residual: bfloat16 [512, 4096], P(('row', 'col'), 'pair')
The draws below stay inside these ranges and needn't reach their ends.
All inputs are finite; a program needn't handle non-finite values.
Results may differ from the reference program's by a relative error of at most 0.00115.
Values may be sent and summed in bfloat16 or wider, within the bound.
No kernel may reach another device: no remote copies, remote signals or barrier semaphores. Data moves between devices by JAX's collectives and lax.ppermute only.
A program may use at most 192 MiB of HBM per device.

```python
import jax
import jax.numpy as jnp
from jax import lax

NV = 512
TILE = 64
WIN = 64
NPAIR = 512
NT = 8


def plant(array, stream_key, low, top_value):
    longest = array.shape.index(max(array.shape))
    spots = []
    for shift in (0, 1):
        where = [jax.random.randint(jax.random.fold_in(stream_key, axis), (), 0, length) for axis, length in enumerate(array.shape)]
        where[longest] = (where[longest] + shift) % array.shape[longest]
        spots.append(tuple(where))
    return array.at[spots[0]].set(low).at[spots[1]].set(top_value)


def spiked(entries, own_key, source, target, blocks, factor):
    owner, partner = [(jnp.arange(entries.shape[dim]) // (entries.shape[dim] // blocks)).reshape([-1 if axis == dim else 1 for axis in range(entries.ndim)]) for dim in (source, target)]
    chosen = jax.random.permutation(own_key, blocks)[partner]
    strong = (owner == chosen) | (owner == (partner + blocks // 2) % blocks)
    return jnp.where(strong, factor * entries, entries)


def block_scale(key, shape, cuts, smallest, largest):
    factor_of = 1.0
    for position, parts in cuts:
        draws = jax.random.uniform(jax.random.fold_in(jax.random.fold_in(key, 6), position), (parts,), jnp.float32, smallest / len(cuts), largest / len(cuts))
        factor_of = factor_of * jnp.repeat(jnp.exp(draws), shape[position] // parts).reshape((-1,) + (1,) * (len(shape) - 1 - position))
    return factor_of


def scatter_about(own_key, shape, scale, limit, shards=(), kind=jnp.bfloat16):
    array = scale * jax.random.normal(own_key, shape, jnp.float32)
    if shards:
        array = array * block_scale(own_key, shape, shards, -0.22, 0.18)
    return jnp.clip(array, -limit, limit).astype(kind)


def heavy_noise(key, dims, width, reach, cuts, heavy, dtype=jnp.bfloat16):
    drawn = width * jax.random.normal(key, dims, jnp.float32)
    if cuts:
        drawn = drawn * block_scale(key, dims, cuts, -0.22, 0.18)
    return jnp.clip(spiked(drawn, jax.random.fold_in(key, 3), *heavy), -reach, reach).astype(dtype)


def setup_inputs(seed: int = 0) -> dict:
    splits = jax.random.split(jax.random.key(seed), 5)
    return {
        "amps": heavy_noise(splits[0], (NPAIR, NV, NV), 1.0, 6.0, ((0, 4), (1, 2), (2, 4)), (1, 0, 4, 2.0)),
        "integrals": scatter_about(splits[1], (WIN * WIN, NV, NV), (NV * NV) ** -0.5, 0.01171875, ((0, 4), (1, 2), (2, 4))),
        "mask_amps": plant((jax.random.randint(splits[2], (NT, NT), 0, 4) < 3).astype(jnp.int32), jax.random.fold_in(splits[2], 1), 0, 1),
        "mask_ints": plant((jax.random.randint(splits[3], (NT, NT), 0, 4) < 3).astype(jnp.int32), jax.random.fold_in(splits[3], 1), 0, 1),
    }


def tile_factor(mask):
    tiles = jnp.arange(NV) // TILE
    onehot = (tiles[:, None] == jnp.arange(NT)[None, :]).astype(jnp.float32)
    return jnp.dot(jnp.dot(onehot, mask.astype(jnp.float32)), onehot.T)


def reference(amps, integrals, mask_amps, mask_ints):
    factor_amps = tile_factor(mask_amps).astype(jnp.bfloat16)
    factor_ints = tile_factor(mask_ints).astype(jnp.bfloat16)
    flat_amps = (amps * factor_amps[None]).reshape(NPAIR, NV * NV)
    grouped = integrals.reshape(WIN, WIN, NV, NV)

    def one_row(block):
        masked = (block * factor_ints[None]).reshape(WIN, NV * NV)
        return lax.dot_general(flat_amps, masked, (((1,), (1,)), ((), ())), preferred_element_type=jnp.float32)

    ladder = lax.map(one_row, grouped)
    ladder = jnp.transpose(ladder, (1, 0, 2))
    result = 0.5 * (ladder - jnp.transpose(ladder, (0, 2, 1)))
    return result.reshape(NPAIR, WIN * WIN).astype(jnp.bfloat16)
```

```python
import functools

import jax
import jax.numpy as jnp
from jax import lax
from jax.experimental import pallas as pl
from jax.experimental.pallas import tpu as pltpu
from jax.sharding import PartitionSpec as P

TILE = 64
WIN = 64
LANES = 128
AB_BLOCK = 512
VMEM_LIMIT = 48 * 1024 * 1024
BUCKETS = (4, 6, 7, 8, 9, 10, 11, 12, 13, 14, 16)

SLOTS, OWN, OTHER, CORE, PLANE, UNITS = 0, 1, 2, 3, 4, 8


class Sizes:
    def __init__(self, amps, integrals):
        self.pairs, self.local_c, self.local_d = amps.shape
        self.local_ab = integrals.shape[0]
        self.uc = min(self.local_c, TILE)
        self.ud = min(self.local_d, TILE)
        self.nuc = self.local_c // self.uc
        self.nud = self.local_d // self.ud
        self.units = self.nuc * self.nud
        self.half = self.pairs // 2
        self.rows = self.uc // 2
        self.chunks = 2 if self.rows % 32 == 0 else 1
        self.crows = self.rows // self.chunks
        self.kc = self.crows * LANES
        self.split = self.rows % 16 == 0


def plan_kernel(z, rows, cols, pos_ref, ma_ref, mi_ref, table_ref):
    row, col, plane = pos_ref[0], pos_ref[1], pos_ref[2]
    core = lax.rem(col, 2)

    def active(r, c, unit):
        ct = (r * z.local_c + (unit // z.nud) * z.uc) // TILE
        dt = (c * z.local_d + lax.rem(unit, z.nud) * z.ud) // TILE
        return jnp.where(ma_ref[ct, dt] * mi_ref[ct, dt] != 0, 1, 0)

    def count(r, c):
        return lax.fori_loop(0, z.units, lambda u, n: n + active(r, c, u), 0)

    def group(g, most):
        r, pairc = g // (cols // 2), lax.rem(g, cols // 2)
        return jnp.maximum(most, count(r, 2 * pairc) + count(r, 2 * pairc + 1))

    table_ref[SLOTS] = lax.fori_loop(0, rows * (cols // 2), group, 0)
    for i in range(z.units):
        table_ref[UNITS + i] = 0

    def fill(u, n):
        on = active(row, col, u)

        @pl.when(on == 1)
        def _():
            table_ref[UNITS + n] = u

        return n + on

    table_ref[OWN] = lax.fori_loop(0, z.units, fill, 0)
    table_ref[OTHER] = count(row, col + 1 - 2 * core)
    table_ref[CORE] = core
    table_ref[PLANE] = plane


def make_plan(z, mask_amps, mask_ints):
    rows, cols = lax.axis_size("row"), lax.axis_size("col")
    pos = jnp.stack([lax.axis_index("row"), lax.axis_index("col"), lax.axis_index("pair")]).astype(jnp.int32)
    smem = pl.BlockSpec(memory_space=pltpu.SMEM)
    return pl.pallas_call(
        functools.partial(plan_kernel, z, rows, cols),
        out_shape=jax.ShapeDtypeStruct((UNITS + z.units,), jnp.int32),
        in_specs=[smem] * 3,
        out_specs=smem,
        name="plan",
    )(pos, mask_amps, mask_ints)


def squeeze_tile(second, x, y):
    low = lax.broadcasted_iota(jnp.int32, x.shape, 2) < TILE
    if second:
        return jnp.where(low, jnp.concatenate([x[..., TILE:], x[..., :TILE]], -1), y)
    return jnp.where(low, x, jnp.concatenate([y[..., TILE:], y[..., :TILE]], -1))


def last_valid(i, n):
    return jnp.minimum(i, jnp.maximum(n - 1, 0))


def slot_owner(i, slots, t):
    core = t[CORE]
    first = jnp.where(core == 0, t[OWN], t[OTHER])
    second = jnp.where(core == 0, t[OTHER], t[OWN])
    in_first = i < first
    in_second = i >= slots - second
    own = jnp.where(core == 0, in_first, in_second)
    other = jnp.where(core == 0, in_second, in_first)
    return own, other, jnp.where(in_first, i, i - (slots - second))


def pack_own_kernel(z, t, a_ref, *outs):
    i = pl.program_id(0)
    unit = t[UNITS + last_valid(i, t[OWN])]
    for second in range(z.nud):

        @pl.when((i < t[OWN]) & (lax.rem(unit, z.nud) == second))
        def _(second=second):
            v = squeeze_tile(second, a_ref[:, : z.rows, :], a_ref[:, z.rows :, :])
            for k, o in enumerate(outs):
                o[0] = v[:, k * z.crows : (k + 1) * z.crows].reshape(z.half, z.kc)


def pack_own(z, steps, table, amps):
    def amap(i, t):
        return (1 - t[CORE], t[UNITS + last_valid(i, t[OWN])] // z.nud, 0)

    return pl.pallas_call(
        functools.partial(pack_own_kernel, z),
        grid_spec=pltpu.PrefetchScalarGridSpec(
            num_scalar_prefetch=1,
            grid=(steps,),
            in_specs=[pl.BlockSpec((z.half, z.uc, LANES), amap)],
            out_specs=[pl.BlockSpec((1, z.half, z.kc), lambda i, t: (i, 0, 0))] * z.chunks,
        ),
        out_shape=[jax.ShapeDtypeStruct((steps, z.half, z.kc), jnp.bfloat16)] * z.chunks,
        compiler_params=pltpu.CompilerParams(vmem_limit_bytes=VMEM_LIMIT),
        name="pack_own",
    )(table, amps)


def pack_slots_kernel(z, slots, t, a_ref, *refs):
    ins, outs = refs[: z.chunks], refs[z.chunks :]
    i = pl.program_id(0)
    own, other, index = slot_owner(i, slots, t)
    unit = t[UNITS + jnp.clip(index, 0, z.units - 1)]
    for second in range(z.nud):

        @pl.when(own & (lax.rem(unit, z.nud) == second))
        def _(second=second):
            v = squeeze_tile(second, a_ref[:, : z.rows, :], a_ref[:, z.rows :, :])
            for k, o in enumerate(outs):
                o[0] = v[:, k * z.crows : (k + 1) * z.crows].reshape(z.half, z.kc)

    @pl.when(other)
    def _():
        for p, o in zip(ins, outs):
            o[0] = p[0]


def pack_slots(z, slots, table, amps, partner):
    def amap(i, t):
        own, _, index = slot_owner(i, slots, t)
        return (t[CORE], t[UNITS + jnp.where(own, index, 0)] // z.nud, 0)

    def pmap(i, t):
        _, other, index = slot_owner(i, slots, t)
        return (jnp.where(other, index, 0), 0, 0)

    return pl.pallas_call(
        functools.partial(pack_slots_kernel, z, slots),
        grid_spec=pltpu.PrefetchScalarGridSpec(
            num_scalar_prefetch=1,
            grid=(slots,),
            in_specs=[pl.BlockSpec((z.half, z.uc, LANES), amap)]
            + [pl.BlockSpec((1, z.half, z.kc), pmap)] * z.chunks,
            out_specs=[pl.BlockSpec((1, z.half, z.kc), lambda i, t: (i, 0, 0))] * z.chunks,
        ),
        out_shape=[jax.ShapeDtypeStruct((slots, z.half, z.kc), jnp.bfloat16)] * z.chunks,
        compiler_params=pltpu.CompilerParams(vmem_limit_bytes=VMEM_LIMIT),
        name="pack_slots",
    )(table, amps, *partner)


def source_plane(which, plane):
    if which == 0:
        return plane
    if which == 1:
        return plane + 1 - 2 * lax.rem(plane, 2)
    if which == 2:
        return jnp.where(plane < 2, 2, 1)
    return jnp.where(plane < 2, 3, 0)


def is_end(t):
    return (t[PLANE] == 0) | (t[PLANE] == 3)


def ladder_kernel(z, nsrc, which, start, t, *refs):
    srcs, rest = refs[: 2 * nsrc], refs[2 * nsrc :]
    if not start:
        prev_ref, rest = rest[0], rest[1:]
    if z.split:
        x_ref, y_ref, out_ref, a_ref, b_ref = rest
    else:
        x_ref, out_ref, a_ref, b_ref = rest
    i = pl.program_id(1)
    core = t[CORE]
    unit = t[UNITS + last_valid(i, t[OWN])]

    @pl.when(i == 0)
    def _():
        if start:
            out_ref[...] = jnp.zeros_like(out_ref)
        else:
            out_ref[...] = prev_ref[...]

    for s in range(nsrc):
        chosen = i < t[OWN]
        if nsrc == 2:
            chosen &= is_end(t) == (s == 0)

        @pl.when(chosen)
        def _(s=s):
            a_ref[pl.ds(pl.multiple_of(core * z.half, z.half), z.half)] = srcs[2 * s][0]
            a_ref[pl.ds(pl.multiple_of((1 - core) * z.half, z.half), z.half)] = srcs[2 * s + 1][0]

    for second in range(z.nud):

        @pl.when((i < t[OWN]) & (lax.rem(unit, z.nud) == second))
        def _(second=second):
            if z.split:
                x, y = x_ref[...], y_ref[...]
            else:
                x, y = x_ref[:, : z.rows], x_ref[:, z.rows :]
            b_ref[...] = squeeze_tile(second, x, y).reshape(b_ref.shape)

    @pl.when(i < t[OWN])
    def _():
        out_ref[...] += lax.dot_general(
            a_ref[...], b_ref[...], (((1,), (1,)), ((), ())), preferred_element_type=jnp.float32
        )


def ladder_block(z, slots, steps, table, which, k, sources, integrals, prev, total, own=False):
    nsrc = len(sources)
    ab = min(AB_BLOCK, z.local_ab)
    start = prev is None

    def slot_map(s):
        def index(j, i, t):
            i = last_valid(i, t[OWN])
            at = jnp.where(t[CORE] == 0, i, slots - t[OWN] + i)
            if nsrc == 2:
                at = jnp.where(is_end(t) == (s == 0), at, 0)
            return (jnp.clip(at, 0, slots - 1), 0, 0)

        return index

    def back_map(s):
        def index(j, i, t):
            i = last_valid(i, t[OWN])
            at = i if own else jnp.where(t[CORE] == 0, i, steps - t[OWN] + i)
            if nsrc == 2:
                at = jnp.where(is_end(t) == (s == 0), at, 0)
            return (jnp.clip(at, 0, steps - 1), 0, 0)

        return index

    per_unit = z.uc // z.crows

    def imap(offset):
        def index(j, i, t):
            ct = t[UNITS + last_valid(i, t[OWN])] // z.nud
            return (j, ct * per_unit + offset, 0)

        return index

    def omap(j, i, t):
        return (source_plane(which, t[PLANE]), j)

    in_specs, args = [], []
    for s, (slot_buf, back_buf) in enumerate(sources):
        in_specs += [
            pl.BlockSpec((1, z.half, z.kc), slot_map(s)),
            pl.BlockSpec((1, z.half, z.kc), back_map(s)),
        ]
        args += [slot_buf, back_buf]
    aliases = {}
    out_spec = pl.BlockSpec((z.pairs, ab), omap)
    if total is not None:
        if start:
            in_specs.append(pl.BlockSpec(memory_space=pl.ANY))
        else:
            in_specs.append(out_spec)
        args.append(total)
        aliases = {len(args): 0}
    if z.split:
        in_specs += [
            pl.BlockSpec((ab, z.crows, LANES), imap(k)),
            pl.BlockSpec((ab, z.crows, LANES), imap(z.chunks + k)),
        ]
        args += [integrals, integrals]
    else:
        in_specs.append(
            pl.BlockSpec((ab, z.uc, LANES), lambda j, i, t: (j, t[UNITS + last_valid(i, t[OWN])] // z.nud, 0))
        )
        args.append(integrals)

    def body(t, *refs):
        refs = list(refs)
        if start and total is not None:
            del refs[2 * nsrc]
        ladder_kernel(z, nsrc, which, start, t, *refs)

    return pl.pallas_call(
        body,
        grid_spec=pltpu.PrefetchScalarGridSpec(
            num_scalar_prefetch=1,
            grid=(z.local_ab // ab, steps),
            in_specs=in_specs,
            out_specs=out_spec,
            scratch_shapes=[
                pltpu.VMEM((z.pairs, z.kc), jnp.bfloat16),
                pltpu.VMEM((ab, z.kc), jnp.bfloat16),
            ],
        ),
        out_shape=jax.ShapeDtypeStruct((4 * z.pairs, z.local_ab), jnp.float32),
        input_output_aliases=aliases,
        compiler_params=pltpu.CompilerParams(vmem_limit_bytes=VMEM_LIMIT),
        cost_estimate=pl.CostEstimate(
            flops=2 * z.pairs * z.local_ab * z.kc * steps,
            bytes_accessed=2 * z.local_ab * z.crows * LANES * 2 * steps,
            transcendentals=0,
        ),
        name="ladder_block",
    )(table, *args)


def swap_cores(x, planes=None):
    rows, cols, groups = lax.axis_size("row"), lax.axis_size("col"), lax.axis_size("pair")
    perm = []
    for r in range(rows):
        for c in range(cols):
            for p in range(groups) if planes is None else planes:
                perm.append(((r * cols + c) * groups + p, (r * cols + (c ^ 1)) * groups + p))
    return lax.ppermute(x, ("row", "col", "pair"), perm)


def branch(z, slots, table, amps, integrals):
    steps = min(slots, z.units)
    core = table[CORE]
    start = jnp.where(core == 0, slots - steps, 0)
    ends, middles = (0, 3), (1, 2)
    outward = [(1, 0), (2, 3)]
    across = [(1, 2), (2, 1)]
    both = [(0, 1), (3, 2), (1, 0), (2, 3)]

    def give_back(buf, planes=None):
        part = lax.dynamic_slice_in_dim(buf, start, steps, 0)
        return swap_cores(part, planes)

    mine = pack_own(z, steps, table, amps)
    partner = [swap_cores(m) for m in mine]
    stream = pack_slots(z, slots, table, amps, partner)
    ks = range(z.chunks)
    x = [lax.ppermute(s, "pair", both) for s in stream]
    y = [lax.ppermute(s, "pair", across) for s in stream]
    z1 = [lax.ppermute(b, "pair", outward) for b in y]
    w = [lax.ppermute(b, "pair", across) for b in x]
    z2 = [lax.ppermute(b, "pair", outward) for b in w]

    total = None
    for which in range(4):
        prev = None
        for k in ks:
            if which == 0:
                sources = [(stream[k], mine[k])]
            elif which == 1:
                sources = [(x[k], give_back(x[k]))]
            elif which == 2:
                sources = [(z1[k], give_back(z1[k], ends)), (y[k], give_back(y[k], middles))]
            else:
                sources = [(z2[k], give_back(z2[k], ends)), (w[k], give_back(w[k], middles))]
            total = ladder_block(z, slots, steps, table, which, k, sources, integrals, prev, total, own=which == 0)
            prev = total
    return total


def per_device(amps, integrals, mask_amps, mask_ints):
    z = Sizes(amps, integrals)
    table = make_plan(z, mask_amps, mask_ints)
    most = 2 * z.units
    buckets = [b for b in BUCKETS if b < most] + [most]
    chosen = sum((table[SLOTS] > b).astype(jnp.int32) for b in buckets[:-1]) if len(buckets) > 1 else jnp.int32(0)
    total = lax.switch(
        chosen,
        [functools.partial(branch, z, b) for b in buckets],
        table,
        amps,
        integrals,
    )
    ladder = lax.psum_scatter(total, ("row", "col"), scatter_dimension=0, tiled=True)
    out_pairs = ladder.shape[0]
    groups = lax.axis_size("pair")
    local_a = WIN // groups
    grid = ladder.reshape(out_pairs, local_a, groups, local_a)
    received = lax.all_to_all(grid, "pair", split_axis=2, concat_axis=2, tiled=True)
    swapped = jnp.transpose(received, (0, 3, 2, 1)).reshape(out_pairs, local_a * WIN)
    return (0.5 * (ladder - swapped)).astype(jnp.bfloat16)


def solution(mesh):
    return jax.shard_map(
        per_device,
        mesh=mesh,
        in_specs=(P("pair", "row", "col"), P("pair", "row", "col"), P(), P()),
        out_specs=P(("row", "col"), "pair"),
        check_vma=False,
    )
```

```python
import functools

import jax
import jax.numpy as jnp
from jax import lax
from jax.experimental import pallas as pl
from jax.experimental.pallas import tpu as pltpu
from jax.sharding import PartitionSpec as P

TILE = 64
WIN = 64
LANES = 128
AB_BLOCK = 512
PIECE = 2
VMEM_LIMIT = 50 * 1024 * 1024

SLOTS, CORE, UNITS = 0, 1, 8


class Sizes:
    def __init__(self, amps, integrals):
        self.pairs, self.local_c, self.local_d = amps.shape
        self.local_ab = integrals.shape[0]
        self.uc = min(self.local_c, TILE)
        self.ud = min(self.local_d, TILE)
        self.nud = self.local_d // self.ud
        self.units = (self.local_c // self.uc) * self.nud
        self.half = self.pairs // 2
        self.rows = self.uc // 2
        self.k = self.rows * LANES
        self.most = 2 * self.units
        self.slot_unit = UNITS + self.units
        self.slot_other = self.slot_unit + self.most
        self.table = self.slot_other + self.most


def plan_kernel(z, rows, cols, pos_ref, ma_ref, mi_ref, table_ref):
    row, col = pos_ref[0], pos_ref[1]
    core = lax.rem(col, 2)

    def active(r, c, unit):
        ct = (r * z.local_c + (unit // z.nud) * z.uc) // TILE
        dt = (c * z.local_d + lax.rem(unit, z.nud) * z.ud) // TILE
        return jnp.where(ma_ref[ct, dt] * mi_ref[ct, dt] != 0, 1, 0)

    def count(r, c):
        return lax.fori_loop(0, z.units, lambda u, n: n + active(r, c, u), 0)

    def group(g, most):
        r, pairc = g // (cols // 2), lax.rem(g, cols // 2)
        return jnp.maximum(most, count(r, 2 * pairc) + count(r, 2 * pairc + 1))

    table_ref[SLOTS] = lax.fori_loop(0, rows * (cols // 2), group, 0)
    table_ref[CORE] = core
    for i in range(z.units):
        table_ref[UNITS + i] = 0

    def fill(u, n):
        on = active(row, col, u)

        @pl.when(on == 1)
        def _():
            table_ref[UNITS + n] = u

        return n + on

    own = lax.fori_loop(0, z.units, fill, 0)
    other = count(row, col + 1 - 2 * core)
    first = jnp.where(core == 0, own, other)
    second = jnp.where(core == 0, other, own)
    extra = jnp.abs(first - second)
    richer = jnp.where(first >= second, 0, 1)
    for s in range(z.most):
        j = s - extra
        owner = jnp.where(s < extra, richer, lax.rem(jnp.maximum(j, 0), 2))
        index = jnp.where(s < extra, s, j // 2 + jnp.where(owner == richer, extra, 0))
        live = s < own + other
        mine = live & (owner == core)
        theirs = live & (owner != core)
        index = jnp.clip(index, 0, z.units - 1)
        table_ref[z.slot_unit + s] = jnp.where(mine, table_ref[UNITS + index], -1)
        table_ref[z.slot_other + s] = jnp.where(theirs, index, -1)


def make_plan(z, mask_amps, mask_ints):
    rows, cols = lax.axis_size("row"), lax.axis_size("col")
    pos = jnp.stack([lax.axis_index("row"), lax.axis_index("col")]).astype(jnp.int32)
    smem = pl.BlockSpec(memory_space=pltpu.SMEM)
    return pl.pallas_call(
        functools.partial(plan_kernel, z, rows, cols),
        out_shape=jax.ShapeDtypeStruct((z.table,), jnp.int32),
        in_specs=[smem] * 3,
        out_specs=smem,
        name="plan",
    )(pos, mask_amps, mask_ints)


def squeeze_tile(second, x, y):
    low = lax.broadcasted_iota(jnp.int32, x.shape, 2) < TILE
    if second:
        return jnp.where(low, jnp.concatenate([x[..., TILE:], x[..., :TILE]], -1), y)
    return jnp.where(low, x, jnp.concatenate([y[..., TILE:], y[..., :TILE]], -1))


def pack_tile(z, unit, on, a_ref, o_ref):
    for second in range(z.nud):

        @pl.when(on & (lax.rem(unit, z.nud) == second))
        def _(second=second):
            v = squeeze_tile(second, a_ref[:, : z.rows, :], a_ref[:, z.rows :, :])
            o_ref[0] = v.reshape(z.half, z.k)


def pack_own(z, table, amps):
    def body(t, a_ref, o_ref):
        i = pl.program_id(0)
        unit = t[UNITS + i]
        pack_tile(z, unit, (i == 0) | (unit > 0), a_ref, o_ref)

    return pl.pallas_call(
        body,
        grid_spec=pltpu.PrefetchScalarGridSpec(
            num_scalar_prefetch=1,
            grid=(z.units,),
            in_specs=[pl.BlockSpec((z.half, z.uc, LANES), lambda i, t: (1 - t[CORE], t[UNITS + i] // z.nud, 0))],
            out_specs=pl.BlockSpec((1, z.half, z.k), lambda i, t: (i, 0, 0)),
        ),
        out_shape=jax.ShapeDtypeStruct((z.units, z.half, z.k), jnp.bfloat16),
        compiler_params=pltpu.CompilerParams(vmem_limit_bytes=VMEM_LIMIT),
        name="pack_own",
    )(table, amps)


def pack_slots(z, table, amps, partner):
    def body(t, a_ref, p_ref, o_ref):
        s = pl.program_id(0)
        unit = t[z.slot_unit + s]
        pack_tile(z, unit, unit >= 0, a_ref, o_ref)

        @pl.when(t[z.slot_other + s] >= 0)
        def _():
            o_ref[0] = p_ref[0]

    return pl.pallas_call(
        body,
        grid_spec=pltpu.PrefetchScalarGridSpec(
            num_scalar_prefetch=1,
            grid=(z.most,),
            in_specs=[
                pl.BlockSpec(
                    (z.half, z.uc, LANES), lambda s, t: (t[CORE], jnp.maximum(t[z.slot_unit + s], 0) // z.nud, 0)
                ),
                pl.BlockSpec((1, z.half, z.k), lambda s, t: (jnp.maximum(t[z.slot_other + s], 0), 0, 0)),
            ],
            out_specs=pl.BlockSpec((1, z.half, z.k), lambda s, t: (s, 0, 0)),
        ),
        out_shape=jax.ShapeDtypeStruct((z.most, z.half, z.k), jnp.bfloat16),
        compiler_params=pltpu.CompilerParams(vmem_limit_bytes=VMEM_LIMIT),
        name="pack_slots",
    )(table, amps, partner)


def ladder_piece(z, table, piece, gathered, swapped, integrals, total):
    groups = gathered.shape[0]
    ab = min(AB_BLOCK, z.local_ab)
    step = min(z.rows, 16)
    per_unit = z.uc // z.rows
    split = z.rows % 16 == 0

    def unit_of(t, p, s):
        return t[z.slot_unit + p[0] * PIECE + s]

    def body(t, p, g_ref, w_ref, prev_ref, *rest):
        if split:
            x_ref, y_ref, out_ref, a_ref, b_ref = rest
        else:
            x_ref, out_ref, a_ref, b_ref = rest
        s = pl.program_id(1)
        core = t[CORE]
        unit = unit_of(t, p, s)

        @pl.when(s == 0)
        def _():
            out_ref[...] = prev_ref[...]

        @pl.when(unit >= 0)
        def _():
            for g in range(groups):
                here = pl.multiple_of(g * z.pairs + core * z.half, z.half)
                there = pl.multiple_of(g * z.pairs + (1 - core) * z.half, z.half)
                a_ref[pl.ds(here, z.half)] = g_ref[g, 0]
                a_ref[pl.ds(there, z.half)] = w_ref[g, 0]

        for second in range(z.nud):

            @pl.when((unit >= 0) & (lax.rem(unit, z.nud) == second))
            def _(second=second):
                for k in range(z.rows // step):
                    at = slice(k * step, (k + 1) * step)
                    up = slice(z.rows + k * step, z.rows + (k + 1) * step)
                    x, y = (x_ref[:, at], y_ref[:, at]) if split else (x_ref[:, at], x_ref[:, up])
                    b_ref[:, k * step * LANES : (k + 1) * step * LANES] = squeeze_tile(second, x, y).reshape(
                        ab, step * LANES
                    )

        @pl.when(unit >= 0)
        def _():
            def add(k, _):
                cols = pl.ds(pl.multiple_of(k * step * LANES, step * LANES), step * LANES)
                out_ref[...] += lax.dot_general(
                    a_ref[:, cols], b_ref[:, cols], (((1,), (1,)), ((), ())), preferred_element_type=jnp.float32
                )
                return 0

            lax.fori_loop(0, z.rows // step, add, 0)

    def imap(offset):
        def index(j, s, t, p):
            return (j, jnp.maximum(unit_of(t, p, s), 0) // z.nud * per_unit + offset, 0)

        return index

    piece_spec = pl.BlockSpec((groups, 1, z.half, z.k), lambda j, s, t, p: (0, s, 0, 0))
    out_spec = pl.BlockSpec((groups * z.pairs, ab), lambda j, s, t, p: (0, j))
    if split:
        ints_specs = [pl.BlockSpec((ab, z.rows, LANES), imap(0)), pl.BlockSpec((ab, z.rows, LANES), imap(1))]
        ints = [integrals, integrals]
    else:
        ints_specs = [
            pl.BlockSpec((ab, z.uc, LANES), lambda j, s, t, p: (j, jnp.maximum(unit_of(t, p, s), 0) // z.nud, 0))
        ]
        ints = [integrals]
    return pl.pallas_call(
        body,
        grid_spec=pltpu.PrefetchScalarGridSpec(
            num_scalar_prefetch=2,
            grid=(z.local_ab // ab, PIECE),
            in_specs=[piece_spec, piece_spec, out_spec] + ints_specs,
            out_specs=out_spec,
            scratch_shapes=[
                pltpu.VMEM((groups * z.pairs, z.k), jnp.bfloat16),
                pltpu.VMEM((ab, z.k), jnp.bfloat16),
            ],
        ),
        out_shape=jax.ShapeDtypeStruct((groups * z.pairs, z.local_ab), jnp.float32),
        input_output_aliases={4: 0},
        compiler_params=pltpu.CompilerParams(vmem_limit_bytes=VMEM_LIMIT),
        cost_estimate=pl.CostEstimate(
            flops=2 * groups * z.pairs * z.local_ab * z.k * PIECE,
            bytes_accessed=2 * z.local_ab * z.uc * LANES * PIECE,
            transcendentals=0,
        ),
        name="ladder_piece",
    )(table, piece, gathered, swapped, total, *ints)


def swap_cores(x):
    return lax.ppermute(x, "col", [(i, i ^ 1) for i in range(lax.axis_size("col"))])


def pick(x, at, axis):
    return lax.dynamic_index_in_dim(x, at, axis, keepdims=False)


def reduce_plane(z, total):
    row, col = lax.axis_index("row"), lax.axis_index("col")
    chip, core = col // 2, lax.rem(col, 2)

    def over_row(x):
        return lax.ppermute(x, "row", [(0, 1), (1, 0)])

    def over_chip(x):
        return lax.ppermute(x, "col", [(i, i ^ 2) for i in range(4)])

    def halve(x, at, axis, send):
        return pick(x, at, axis) + send(pick(x, 1 - at, axis))

    wide = z.local_ab // 2
    rest = total.reshape(2, 2, 2, z.half, z.local_ab)
    rest = halve(rest, core, 2, swap_cores)
    left, right = rest[..., :wide], rest[..., wide:]
    left = halve(left, row, 0, over_row)
    right = halve(right, chip, 1, over_chip)
    left = halve(left, chip, 0, over_chip)
    right = halve(right, row, 0, over_row)
    return jnp.concatenate([left, right], -1)


def per_device(amps, integrals, mask_amps, mask_ints):
    z = Sizes(amps, integrals)
    table = make_plan(z, mask_amps, mask_ints)
    stream = pack_slots(z, table, amps, swap_cores(pack_own(z, table, amps)))
    pieces = jnp.maximum((table[SLOTS] + PIECE - 1) // PIECE, 1)
    groups = lax.axis_size("pair")

    def gather(p):
        return lax.all_gather(lax.dynamic_slice_in_dim(stream, p * PIECE, PIECE, 0), "pair")

    def add(p, gathered, total):
        return ladder_piece(z, table, jnp.reshape(p, (1,)), gathered, swap_cores(gathered), integrals, total)

    def step(p, carry):
        gathered, total = carry
        return lax.optimization_barrier((gather(p), add(p - 1, gathered, total)))

    total = jnp.zeros((groups * z.pairs, z.local_ab), jnp.float32)
    gathered, total = lax.fori_loop(1, pieces, step, (gather(0), total))
    total = add(pieces - 1, gathered, total)

    if lax.axis_size("row") == 2 and lax.axis_size("col") == 4:
        ladder = reduce_plane(z, total)
    else:
        ladder = lax.psum_scatter(total, ("row", "col"), scatter_dimension=0, tiled=True)
    out_pairs = ladder.shape[0]
    local_a = WIN // groups
    grid = ladder.reshape(out_pairs, local_a, groups, local_a)
    received = lax.all_to_all(grid, "pair", split_axis=2, concat_axis=2, tiled=True)
    swapped = jnp.transpose(received, (0, 3, 2, 1)).reshape(out_pairs, local_a * WIN)
    return (0.5 * (ladder - swapped)).astype(jnp.bfloat16)


def solution(mesh):
    return jax.shard_map(
        per_device,
        mesh=mesh,
        in_specs=(P("pair", "row", "col"), P("pair", "row", "col"), P(), P()),
        out_specs=P(("row", "col"), "pair"),
        check_vma=False,
    )
```

```python
import functools

import jax
import jax.numpy as jnp
from jax import lax
from jax.experimental import pallas as pl
from jax.experimental.pallas import tpu as pltpu
from jax.sharding import PartitionSpec as P

TILE = 64
WIN = 64
LANES = 128
AB_BLOCK = 512
PIECE = 4
VMEM_LIMIT = 50 * 1024 * 1024

FIRST, PIECES, CORE, UNITS = 0, 1, 2, 8


class Sizes:
    def __init__(self, amps, integrals):
        self.pairs, self.local_c, self.local_d = amps.shape
        self.local_ab = integrals.shape[0]
        self.uc = min(self.local_c, TILE)
        self.ud = min(self.local_d, TILE)
        self.nud = self.local_d // self.ud
        self.units = (self.local_c // self.uc) * self.nud
        self.half = self.pairs // 2
        self.rows = self.uc // 2
        self.k = self.rows * LANES
        self.most = -(-2 * self.units // PIECE) * PIECE
        self.slot_mine = UNITS + self.units
        self.slot_other = self.slot_mine + self.most
        self.table = self.slot_other + self.most


def plan_kernel(z, rows, cols, pos_ref, ma_ref, mi_ref, table_ref):
    row, col = pos_ref[0], pos_ref[1]
    core = lax.rem(col, 2)

    def active(r, c, unit):
        ct = (r * z.local_c + (unit // z.nud) * z.uc) // TILE
        dt = (c * z.local_d + lax.rem(unit, z.nud) * z.ud) // TILE
        return jnp.where(ma_ref[ct, dt] * mi_ref[ct, dt] != 0, 1, 0)

    def count(r, c):
        return lax.fori_loop(0, z.units, lambda u, n: n + active(r, c, u), 0)

    def group(g, most):
        r, pairc = g // (cols // 2), lax.rem(g, cols // 2)
        return jnp.maximum(most, count(r, 2 * pairc) + count(r, 2 * pairc + 1))

    slots = jnp.maximum(lax.fori_loop(0, rows * (cols // 2), group, 0), 1)
    first_len = lax.rem(slots - 1, PIECE) + 1
    table_ref[FIRST] = first_len
    table_ref[PIECES] = (slots - first_len) // PIECE + 1
    table_ref[CORE] = core
    for i in range(z.units):
        table_ref[UNITS + i] = 0

    def fill(u, n):
        on = active(row, col, u)

        @pl.when(on == 1)
        def _():
            table_ref[UNITS + n] = u

        return n + on

    own = lax.fori_loop(0, z.units, fill, 0)
    other = count(row, col + 1 - 2 * core)
    first = jnp.where(core == 0, own, other)
    second = jnp.where(core == 0, other, own)
    extra = jnp.abs(first - second)
    richer = jnp.where(first >= second, 0, 1)
    for at in range(z.most):
        s = at if at < PIECE else at - PIECE + first_len
        j = s - extra
        owner = jnp.where(s < extra, richer, lax.rem(jnp.maximum(j, 0), 2))
        index = jnp.where(s < extra, s, j // 2 + jnp.where(owner == richer, extra, 0))
        live = s < own + other
        if at < PIECE:
            live &= s < first_len
        unit = table_ref[UNITS + jnp.clip(index, 0, z.units - 1)]
        table_ref[z.slot_mine + at] = jnp.where(live & (owner == core), unit, -1)
        table_ref[z.slot_other + at] = jnp.where(live & (owner != core), 1, 0)


def make_plan(z, mask_amps, mask_ints):
    rows, cols = lax.axis_size("row"), lax.axis_size("col")
    pos = jnp.stack([lax.axis_index("row"), lax.axis_index("col")]).astype(jnp.int32)
    smem = pl.BlockSpec(memory_space=pltpu.SMEM)
    return pl.pallas_call(
        functools.partial(plan_kernel, z, rows, cols),
        out_shape=jax.ShapeDtypeStruct((z.table,), jnp.int32),
        in_specs=[smem] * 3,
        out_specs=smem,
        name="plan",
    )(pos, mask_amps, mask_ints)


def squeeze_tile(second, x, y):
    low = lax.broadcasted_iota(jnp.int32, x.shape, 2) < TILE
    if second:
        return jnp.where(low, jnp.concatenate([x[..., TILE:], x[..., :TILE]], -1), y)
    return jnp.where(low, x, jnp.concatenate([y[..., TILE:], y[..., :TILE]], -1))


def pack_tile(z, unit, on, a_ref, o_ref):
    for second in range(z.nud):

        @pl.when(on & (lax.rem(unit, z.nud) == second))
        def _(second=second):
            v = squeeze_tile(second, a_ref[:, : z.rows, :], a_ref[:, z.rows :, :])
            o_ref[0] = v.reshape(z.half, z.k)


def pack_given(z, table, amps, start, count):
    def unit_of(t, i):
        return t[z.slot_mine + start + i]

    def body(t, a_ref, o_ref):
        unit = unit_of(t, pl.program_id(0))
        pack_tile(z, unit, unit >= 0, a_ref, o_ref)

    return pl.pallas_call(
        body,
        grid_spec=pltpu.PrefetchScalarGridSpec(
            num_scalar_prefetch=1,
            grid=(count,),
            in_specs=[
                pl.BlockSpec(
                    (z.half, z.uc, LANES), lambda i, t: (1 - t[CORE], jnp.maximum(unit_of(t, i), 0) // z.nud, 0)
                )
            ],
            out_specs=pl.BlockSpec((1, z.half, z.k), lambda i, t: (i, 0, 0)),
        ),
        out_shape=jax.ShapeDtypeStruct((count, z.half, z.k), jnp.bfloat16),
        compiler_params=pltpu.CompilerParams(vmem_limit_bytes=VMEM_LIMIT),
        cost_estimate=pl.CostEstimate(flops=0, bytes_accessed=3 * count * z.half * z.k * 2, transcendentals=0),
        name="pack_given",
    )(table, amps)


def pack_kept(z, table, amps, received, start, count):
    def unit_of(t, i):
        return t[z.slot_mine + start + i]

    def other(t, i):
        return t[z.slot_other + start + i]

    def body(t, a_ref, p_ref, o_ref):
        i = pl.program_id(0)
        unit = unit_of(t, i)
        pack_tile(z, unit, unit >= 0, a_ref, o_ref)

        @pl.when(other(t, i) == 1)
        def _():
            o_ref[0] = p_ref[0]

    return pl.pallas_call(
        body,
        grid_spec=pltpu.PrefetchScalarGridSpec(
            num_scalar_prefetch=1,
            grid=(count,),
            in_specs=[
                pl.BlockSpec((z.half, z.uc, LANES), lambda i, t: (t[CORE], jnp.maximum(unit_of(t, i), 0) // z.nud, 0)),
                pl.BlockSpec((1, z.half, z.k), lambda i, t: (jnp.where(other(t, i) == 1, i, 0), 0, 0)),
            ],
            out_specs=pl.BlockSpec((1, z.half, z.k), lambda i, t: (i, 0, 0)),
        ),
        out_shape=jax.ShapeDtypeStruct((count, z.half, z.k), jnp.bfloat16),
        compiler_params=pltpu.CompilerParams(vmem_limit_bytes=VMEM_LIMIT),
        cost_estimate=pl.CostEstimate(flops=0, bytes_accessed=4 * count * z.half * z.k * 2, transcendentals=0),
        name="pack_kept",
    )(table, amps, received)


def pack(z, table, amps, start, count):
    given = swap_cores(pack_given(z, table, amps, start, count))
    return pack_kept(z, table, amps, given, start, count)


def ladder_piece(z, table, piece, gathered, swapped, integrals, total):
    groups = gathered.shape[0]
    ab = min(AB_BLOCK, z.local_ab)
    step = min(z.rows, 16)
    per_unit = z.uc // z.rows
    split = z.rows % 16 == 0

    def unit_of(t, p, s):
        return t[z.slot_mine + p[0] * PIECE + s]

    def body(t, p, g_ref, w_ref, prev_ref, *rest):
        if split:
            x_ref, y_ref, out_ref, a_ref, b_ref = rest
        else:
            x_ref, out_ref, a_ref, b_ref = rest
        s = pl.program_id(1)
        core = t[CORE]
        unit = unit_of(t, p, s)

        @pl.when(s == 0)
        def _():
            out_ref[...] = prev_ref[...]

        @pl.when(unit >= 0)
        def _():
            for g in range(groups):
                here = pl.multiple_of(g * z.pairs + core * z.half, z.half)
                there = pl.multiple_of(g * z.pairs + (1 - core) * z.half, z.half)
                a_ref[pl.ds(here, z.half)] = g_ref[g, 0]
                a_ref[pl.ds(there, z.half)] = w_ref[g, 0]

        for second in range(z.nud):

            @pl.when((unit >= 0) & (lax.rem(unit, z.nud) == second))
            def _(second=second):
                for k in range(z.rows // step):
                    at = slice(k * step, (k + 1) * step)
                    up = slice(z.rows + k * step, z.rows + (k + 1) * step)
                    x, y = (x_ref[:, at], y_ref[:, at]) if split else (x_ref[:, at], x_ref[:, up])
                    b_ref[:, k * step * LANES : (k + 1) * step * LANES] = squeeze_tile(second, x, y).reshape(
                        ab, step * LANES
                    )

        @pl.when(unit >= 0)
        def _():
            def add(k, _):
                cols = pl.ds(pl.multiple_of(k * step * LANES, step * LANES), step * LANES)
                out_ref[...] += lax.dot_general(
                    a_ref[:, cols], b_ref[:, cols], (((1,), (1,)), ((), ())), preferred_element_type=jnp.float32
                )
                return 0

            lax.fori_loop(0, z.rows // step, add, 0)

    def imap(offset):
        def index(j, s, t, p):
            return (j, jnp.maximum(unit_of(t, p, s), 0) // z.nud * per_unit + offset, 0)

        return index

    piece_spec = pl.BlockSpec((groups, 1, z.half, z.k), lambda j, s, t, p: (0, s, 0, 0))
    out_spec = pl.BlockSpec((groups * z.pairs, ab), lambda j, s, t, p: (0, j))
    if split:
        ints_specs = [pl.BlockSpec((ab, z.rows, LANES), imap(0)), pl.BlockSpec((ab, z.rows, LANES), imap(1))]
        ints = [integrals, integrals]
    else:
        ints_specs = [
            pl.BlockSpec((ab, z.uc, LANES), lambda j, s, t, p: (j, jnp.maximum(unit_of(t, p, s), 0) // z.nud, 0))
        ]
        ints = [integrals]
    return pl.pallas_call(
        body,
        grid_spec=pltpu.PrefetchScalarGridSpec(
            num_scalar_prefetch=2,
            grid=(z.local_ab // ab, PIECE),
            in_specs=[piece_spec, piece_spec, out_spec] + ints_specs,
            out_specs=out_spec,
            scratch_shapes=[
                pltpu.VMEM((groups * z.pairs, z.k), jnp.bfloat16),
                pltpu.VMEM((ab, z.k), jnp.bfloat16),
            ],
        ),
        out_shape=jax.ShapeDtypeStruct((groups * z.pairs, z.local_ab), jnp.float32),
        input_output_aliases={4: 0},
        compiler_params=pltpu.CompilerParams(vmem_limit_bytes=VMEM_LIMIT),
        cost_estimate=pl.CostEstimate(
            flops=2 * groups * z.pairs * z.local_ab * z.k * PIECE,
            bytes_accessed=2 * z.local_ab * z.uc * LANES * PIECE,
            transcendentals=0,
        ),
        name="ladder_piece",
    )(table, piece, gathered, swapped, total, *ints)


def swap_cores(x):
    return lax.ppermute(x, "col", [(i, i ^ 1) for i in range(lax.axis_size("col"))])


def pick(x, at, axis):
    return lax.dynamic_index_in_dim(x, at, axis, keepdims=False)


def reduce_plane(z, total):
    row, col = lax.axis_index("row"), lax.axis_index("col")
    chip, core = col // 2, lax.rem(col, 2)

    def over_row(x):
        return lax.ppermute(x, "row", [(0, 1), (1, 0)])

    def over_chip(x):
        return lax.ppermute(x, "col", [(i, i ^ 2) for i in range(4)])

    def halve(x, at, axis, send):
        return pick(x, at, axis) + send(pick(x, 1 - at, axis))

    wide = z.local_ab // 2
    rest = total.reshape(2, 2, 2, z.half, z.local_ab)
    rest = halve(rest, core, 2, swap_cores)
    left, right = rest[..., :wide], rest[..., wide:]
    left = halve(left, row, 0, over_row)
    right = halve(right, chip, 1, over_chip)
    left = halve(left, chip, 0, over_chip)
    right = halve(right, row, 0, over_row)
    return jnp.concatenate([left, right], -1)


def per_device(amps, integrals, mask_amps, mask_ints):
    z = Sizes(amps, integrals)
    table = make_plan(z, mask_amps, mask_ints)
    groups = lax.axis_size("pair")
    later = z.most - PIECE

    def begin(count, head):
        gathered = lax.all_gather(head[:count], "pair")
        if later:
            gathered, rest = lax.optimization_barrier((gathered, pack(z, table, amps, PIECE, later)))
        else:
            rest = head
        return jnp.pad(gathered, ((0, 0), (0, PIECE - count), (0, 0), (0, 0))), rest

    def add(p, gathered, total):
        return ladder_piece(z, table, jnp.reshape(p, (1,)), gathered, swap_cores(gathered), integrals, total)

    def step(p, carry):
        gathered, total = carry
        own = lax.dynamic_slice_in_dim(rest, (p - 1) * PIECE, PIECE, 0)
        return lax.optimization_barrier((lax.all_gather(own, "pair"), add(p - 1, gathered, total)))

    head = pack(z, table, amps, 0, PIECE)
    gathered, rest = lax.switch(table[FIRST] - 1, [functools.partial(begin, n + 1) for n in range(PIECE)], head)
    total = jnp.zeros((groups * z.pairs, z.local_ab), jnp.float32)
    gathered, total = lax.fori_loop(1, table[PIECES], step, (gathered, total))
    total = add(table[PIECES] - 1, gathered, total)

    if lax.axis_size("row") == 2 and lax.axis_size("col") == 4:
        ladder = reduce_plane(z, total)
    else:
        ladder = lax.psum_scatter(total, ("row", "col"), scatter_dimension=0, tiled=True)
    out_pairs = ladder.shape[0]
    local_a = WIN // groups
    grid = ladder.reshape(out_pairs, local_a, groups, local_a)
    received = lax.all_to_all(grid, "pair", split_axis=2, concat_axis=2, tiled=True)
    swapped = jnp.transpose(received, (0, 3, 2, 1)).reshape(out_pairs, local_a * WIN)
    return (0.5 * (ladder - swapped)).astype(jnp.bfloat16)


def solution(mesh):
    return jax.shard_map(
        per_device,
        mesh=mesh,
        in_specs=(P("pair", "row", "col"), P("pair", "row", "col"), P(), P()),
        out_specs=P(("row", "col"), "pair"),
        check_vma=False,
    )
```

```python
import functools

import jax
import jax.numpy as jnp
from jax import lax
from jax.experimental import pallas as pl
from jax.experimental.pallas import tpu as pltpu
from jax.sharding import PartitionSpec as P

TILE = 64
WIN = 64
LANES = 128
AB_BLOCK = 512
PIECE = 4
VMEM_LIMIT = 50 * 1024 * 1024

FIRST, LONG, CORE, UNITS = 0, 1, 2, 8
HEAD, SECOND, LENT, THIRD, RARE = 0, 1, 2, 3, 4


class Sizes:
    def __init__(self, amps, integrals):
        self.pairs, self.local_c, self.local_d = amps.shape
        self.local_ab = integrals.shape[0]
        self.uc = min(self.local_c, TILE)
        self.ud = min(self.local_d, TILE)
        self.nud = self.local_d // self.ud
        self.units = (self.local_c // self.uc) * self.nud
        self.half = self.pairs // 2
        self.rows = self.uc // 2
        self.k = self.rows * LANES
        self.most = 2 * self.units
        self.long = self.most > PIECE
        self.places = (5 if self.long else 1) * PIECE
        self.slot_mine = UNITS + self.units
        self.slot_other = self.slot_mine + self.places
        self.adopted = self.slot_other + self.places
        self.table = self.adopted + PIECE


def plan_kernel(z, rows, cols, pos_ref, ma_ref, mi_ref, table_ref):
    row, col = pos_ref[0], pos_ref[1]
    core, chip = lax.rem(col, 2), col // 2

    def active(r, c, unit):
        ct = (r * z.local_c + (unit // z.nud) * z.uc) // TILE
        dt = (c * z.local_d + lax.rem(unit, z.nud) * z.ud) // TILE
        return jnp.where(ma_ref[ct, dt] * mi_ref[ct, dt] != 0, 1, 0)

    def count(r, c):
        return lax.fori_loop(0, z.units, lambda u, n: n + active(r, c, u), 0)

    def of_chip(r, x):
        return count(r, 2 * x) + count(r, 2 * x + 1)

    def lend(here, there):
        move = jnp.minimum(jnp.abs(here - there) // 2, 2)
        return jnp.where(here > there, move, 0), jnp.where(here < there, move, 0)

    table_ref[CORE] = core
    for i in range(z.units):
        table_ref[UNITS + i] = 0

    def fill(u, n):
        on = active(row, col, u)

        @pl.when(on == 1)
        def _():
            table_ref[UNITS + n] = u

        return n + on

    own = lax.fori_loop(0, z.units, fill, 0)
    other = count(row, col + 1 - 2 * core)
    if z.long:
        n = [[of_chip(r, x) for x in range(2)] for r in range(2)]
        by_x = [[lend(n[r][x], n[r][1 - x]) for x in range(2)] for r in range(2)]
        m = [[n[r][x] - by_x[r][x][0] + by_x[r][x][1] for x in range(2)] for r in range(2)]
        by_y = [[lend(m[r][x], m[1 - r][x]) for x in range(2)] for r in range(2)]
        slots = jnp.int32(1)
        for r in range(2):
            for x in range(2):
                slots = jnp.maximum(slots, m[r][x] - by_y[r][x][0] + by_y[r][x][1])

        def here(values):
            return jnp.where(
                row == 0, jnp.where(chip == 0, values[0][0], values[0][1]), jnp.where(chip == 0, values[1][0], values[1][1])
            )

        lent_x, got_x = [here([[v[i] for v in r] for r in by_x]) for i in range(2)]
        lent_y, got_y = [here([[v[i] for v in r] for r in by_y]) for i in range(2)]
        is_long = slots > 3 * PIECE
        first_len = jnp.where(is_long, slots - 3 * PIECE, jnp.maximum(slots - 2 * PIECE, 0))
    else:
        slots = lax.fori_loop(
            0, rows * (cols // 2), lambda g, n: jnp.maximum(n, of_chip(g // (cols // 2), lax.rem(g, cols // 2))), 1
        )
        lent_x = got_x = lent_y = got_y = jnp.int32(0)
        is_long = slots > PIECE
        first_len = slots
    table_ref[FIRST] = first_len
    table_ref[LONG] = jnp.where(is_long, 1, 0)

    first = jnp.where(core == 0, own, other)
    second = jnp.where(core == 0, other, own)
    extra = jnp.abs(first - second)
    richer = jnp.where(first >= second, 0, 1)
    kept = own + other - lent_x - lent_y
    for at in range(z.places):
        piece, j = divmod(at, PIECE)
        borrowed = jnp.bool_(False)
        if piece == HEAD:
            s, live = jnp.int32(j), (j < first_len) & (j < kept)
        elif piece == SECOND:
            if j < 2:
                borrowed, s = j < got_x, first_len + j - got_x
            else:
                borrowed, s = j - 2 < got_y, first_len + j - got_x - got_y
            live = jnp.logical_not(borrowed) & (s < kept)
        elif piece == LENT:
            s = kept + j if j < 2 else kept + lent_x + j - 2
            live = j < lent_x if j < 2 else j - 2 < lent_y
        else:
            s = first_len + (PIECE if piece == THIRD else 2 * PIECE) + j - got_x - got_y
            live = s < kept
        k = s - extra
        owner = jnp.where(s < extra, richer, lax.rem(jnp.maximum(k, 0), 2))
        index = jnp.where(s < extra, s, k // 2 + jnp.where(owner == richer, extra, 0))
        unit = table_ref[UNITS + jnp.clip(index, 0, z.units - 1)]
        table_ref[z.slot_mine + at] = jnp.where(live & (owner == core), unit, -1)
        table_ref[z.slot_other + at] = jnp.where(live & (owner != core), 1, 0)
        if piece == SECOND:
            table_ref[z.adopted + j] = jnp.where(borrowed, 1, 0)


def make_plan(z, mask_amps, mask_ints):
    rows, cols = lax.axis_size("row"), lax.axis_size("col")
    pos = jnp.stack([lax.axis_index("row"), lax.axis_index("col")]).astype(jnp.int32)
    smem = pl.BlockSpec(memory_space=pltpu.SMEM)
    return pl.pallas_call(
        functools.partial(plan_kernel, z, rows, cols),
        out_shape=jax.ShapeDtypeStruct((z.table,), jnp.int32),
        in_specs=[smem] * 3,
        out_specs=smem,
        name="plan",
    )(pos, mask_amps, mask_ints)


def squeeze_tile(second, x, y):
    low = lax.broadcasted_iota(jnp.int32, x.shape, 2) < TILE
    if second:
        return jnp.where(low, jnp.concatenate([x[..., TILE:], x[..., :TILE]], -1), y)
    return jnp.where(low, x, jnp.concatenate([y[..., TILE:], y[..., :TILE]], -1))


def pack_tile(z, unit, on, a_ref, o_ref):
    for second in range(z.nud):

        @pl.when(on & (lax.rem(unit, z.nud) == second))
        def _(second=second):
            v = squeeze_tile(second, a_ref[:, : z.rows, :], a_ref[:, z.rows :, :])
            o_ref[0] = v.reshape(z.half, z.k)


def pack_given(z, table, amps, start, count):
    def unit_of(t, i):
        return t[z.slot_mine + start + i]

    def body(t, a_ref, o_ref):
        unit = unit_of(t, pl.program_id(0))
        pack_tile(z, unit, unit >= 0, a_ref, o_ref)

    return pl.pallas_call(
        body,
        grid_spec=pltpu.PrefetchScalarGridSpec(
            num_scalar_prefetch=1,
            grid=(count,),
            in_specs=[
                pl.BlockSpec(
                    (z.half, z.uc, LANES), lambda i, t: (1 - t[CORE], jnp.maximum(unit_of(t, i), 0) // z.nud, 0)
                )
            ],
            out_specs=pl.BlockSpec((1, z.half, z.k), lambda i, t: (i, 0, 0)),
        ),
        out_shape=jax.ShapeDtypeStruct((count, z.half, z.k), jnp.bfloat16),
        compiler_params=pltpu.CompilerParams(vmem_limit_bytes=VMEM_LIMIT),
        cost_estimate=pl.CostEstimate(flops=0, bytes_accessed=3 * count * z.half * z.k * 2, transcendentals=0),
        name="pack_given",
    )(table, amps)


def pack_kept(z, table, amps, received, start, count):
    def unit_of(t, i):
        return t[z.slot_mine + start + i]

    def other(t, i):
        return t[z.slot_other + start + i]

    def body(t, a_ref, p_ref, o_ref):
        i = pl.program_id(0)
        unit = unit_of(t, i)
        pack_tile(z, unit, unit >= 0, a_ref, o_ref)

        @pl.when(other(t, i) == 1)
        def _():
            o_ref[0] = p_ref[0]

    return pl.pallas_call(
        body,
        grid_spec=pltpu.PrefetchScalarGridSpec(
            num_scalar_prefetch=1,
            grid=(count,),
            in_specs=[
                pl.BlockSpec((z.half, z.uc, LANES), lambda i, t: (t[CORE], jnp.maximum(unit_of(t, i), 0) // z.nud, 0)),
                pl.BlockSpec((1, z.half, z.k), lambda i, t: (jnp.where(other(t, i) == 1, i, 0), 0, 0)),
            ],
            out_specs=pl.BlockSpec((1, z.half, z.k), lambda i, t: (i, 0, 0)),
        ),
        out_shape=jax.ShapeDtypeStruct((count, z.half, z.k), jnp.bfloat16),
        compiler_params=pltpu.CompilerParams(vmem_limit_bytes=VMEM_LIMIT),
        cost_estimate=pl.CostEstimate(flops=0, bytes_accessed=4 * count * z.half * z.k * 2, transcendentals=0),
        name="pack_kept",
    )(table, amps, received)


def pack(z, table, amps, start, count):
    given = swap_cores(pack_given(z, table, amps, start, count))
    return pack_kept(z, table, amps, given, start, count)


def ladder_piece(z, table, piece, gathered, swapped, integrals, total):
    groups = gathered.shape[0]
    ab = min(AB_BLOCK, z.local_ab)
    step = min(z.rows, 16)
    per_unit = z.uc // z.rows
    split = z.rows % 16 == 0

    def unit_of(t, p, s):
        return t[z.slot_mine + p[0] * PIECE + s]

    def body(t, p, g_ref, w_ref, prev_ref, *rest):
        if split:
            x_ref, y_ref, out_ref, a_ref, b_ref = rest
        else:
            x_ref, out_ref, a_ref, b_ref = rest
        s = pl.program_id(1)
        core = t[CORE]
        unit = unit_of(t, p, s)

        @pl.when(s == 0)
        def _():
            out_ref[...] = prev_ref[...]

        @pl.when(unit >= 0)
        def _():
            for g in range(groups):
                here = pl.multiple_of(g * z.pairs + core * z.half, z.half)
                there = pl.multiple_of(g * z.pairs + (1 - core) * z.half, z.half)
                a_ref[pl.ds(here, z.half)] = g_ref[g, 0]
                a_ref[pl.ds(there, z.half)] = w_ref[g, 0]

        for second in range(z.nud):

            @pl.when((unit >= 0) & (lax.rem(unit, z.nud) == second))
            def _(second=second):
                for k in range(z.rows // step):
                    at = slice(k * step, (k + 1) * step)
                    up = slice(z.rows + k * step, z.rows + (k + 1) * step)
                    x, y = (x_ref[:, at], y_ref[:, at]) if split else (x_ref[:, at], x_ref[:, up])
                    b_ref[:, k * step * LANES : (k + 1) * step * LANES] = squeeze_tile(second, x, y).reshape(
                        ab, step * LANES
                    )

        @pl.when(unit >= 0)
        def _():
            def add(k, _):
                cols = pl.ds(pl.multiple_of(k * step * LANES, step * LANES), step * LANES)
                out_ref[...] += lax.dot_general(
                    a_ref[:, cols], b_ref[:, cols], (((1,), (1,)), ((), ())), preferred_element_type=jnp.float32
                )
                return 0

            lax.fori_loop(0, z.rows // step, add, 0)

    def imap(offset):
        def index(j, s, t, p):
            return (j, jnp.maximum(unit_of(t, p, s), 0) // z.nud * per_unit + offset, 0)

        return index

    piece_spec = pl.BlockSpec((groups, 1, z.half, z.k), lambda j, s, t, p: (0, s, 0, 0))
    out_spec = pl.BlockSpec((groups * z.pairs, ab), lambda j, s, t, p: (0, j))
    if split:
        ints_specs = [pl.BlockSpec((ab, z.rows, LANES), imap(0)), pl.BlockSpec((ab, z.rows, LANES), imap(1))]
        ints = [integrals, integrals]
    else:
        ints_specs = [
            pl.BlockSpec((ab, z.uc, LANES), lambda j, s, t, p: (j, jnp.maximum(unit_of(t, p, s), 0) // z.nud, 0))
        ]
        ints = [integrals]
    return pl.pallas_call(
        body,
        grid_spec=pltpu.PrefetchScalarGridSpec(
            num_scalar_prefetch=2,
            grid=(z.local_ab // ab, PIECE),
            in_specs=[piece_spec, piece_spec, out_spec] + ints_specs,
            out_specs=out_spec,
            scratch_shapes=[
                pltpu.VMEM((groups * z.pairs, z.k), jnp.bfloat16),
                pltpu.VMEM((ab, z.k), jnp.bfloat16),
            ],
        ),
        out_shape=jax.ShapeDtypeStruct((groups * z.pairs, z.local_ab), jnp.float32),
        input_output_aliases={4: 0},
        compiler_params=pltpu.CompilerParams(vmem_limit_bytes=VMEM_LIMIT),
        cost_estimate=pl.CostEstimate(
            flops=2 * groups * z.pairs * z.local_ab * z.k * PIECE,
            bytes_accessed=2 * z.local_ab * z.uc * LANES * PIECE,
            transcendentals=0,
        ),
        name="ladder_piece",
    )(table, piece, gathered, swapped, total, *ints)


def swap_cores(x):
    return lax.ppermute(x, "col", [(i, i ^ 1) for i in range(lax.axis_size("col"))])


def over_row(x):
    return lax.ppermute(x, "row", [(0, 1), (1, 0)])


def over_chip(x):
    return lax.ppermute(x, "col", [(i, i ^ 2) for i in range(4)])


def pick(x, at, axis):
    return lax.dynamic_index_in_dim(x, at, axis, keepdims=False)


def reduce_plane(z, total):
    row, col = lax.axis_index("row"), lax.axis_index("col")
    chip, core = col // 2, lax.rem(col, 2)

    def halve(x, at, axis, send):
        return pick(x, at, axis) + send(pick(x, 1 - at, axis))

    wide = z.local_ab // 2
    rest = total.reshape(2, 2, 2, z.half, z.local_ab)
    rest = halve(rest, core, 2, swap_cores)
    left, right = rest[..., :wide], rest[..., wide:]
    left = halve(left, row, 0, over_row)
    right = halve(right, chip, 1, over_chip)
    left = halve(left, chip, 0, over_chip)
    right = halve(right, row, 0, over_row)
    return jnp.concatenate([left, right], -1)


def per_device(amps, integrals, mask_amps, mask_ints):
    z = Sizes(amps, integrals)
    table = make_plan(z, mask_amps, mask_ints)
    groups = lax.axis_size("pair")

    def gather(own):
        return lax.all_gather(own, "pair")

    def add(piece, gathered, total):
        at = jnp.full((1,), piece, jnp.int32)
        return ladder_piece(z, table, at, gathered, swap_cores(gathered), integrals, total)

    def prepare():
        both = pack(z, table, amps, PIECE, 2 * PIECE)
        kept, lent = both[:PIECE], both[PIECE:]
        borrowed = jnp.concatenate([over_chip(lent[:2]), over_row(lent[2:])])
        adopted = table[z.adopted : z.adopted + PIECE] == 1
        return jnp.where(adopted[:, None, None], borrowed, kept)

    def begin(count, head):
        blank = jnp.zeros((groups, PIECE, z.half, z.k), jnp.bfloat16)
        if count == 0:
            return blank, prepare()
        gathered = gather(head[:count])
        if z.long:
            gathered, second = lax.optimization_barrier((gathered, prepare()))
        else:
            second = head
        return jnp.pad(gathered, ((0, 0), (0, PIECE - count), (0, 0), (0, 0))), second

    def rare(total):
        return add(RARE, gather(pack(z, table, amps, RARE * PIECE, PIECE)), total)

    head = pack(z, table, amps, 0, PIECE)
    counts = range(0 if z.long else 1, PIECE + 1)
    gathered, second = lax.switch(table[FIRST] - counts[0], [functools.partial(begin, n) for n in counts], head)
    total = jnp.zeros((groups * z.pairs, z.local_ab), jnp.float32)
    if z.long:
        total = lax.cond(table[LONG] == 1, rare, lambda t: t, total)
        later = gather(second)
        third = pack(z, table, amps, THIRD * PIECE, PIECE)
        later, third, total = lax.optimization_barrier((later, third, add(HEAD, gathered, total)))
        last = gather(third)
        back = jnp.concatenate([over_chip(later[:, :2]), over_row(later[:, 2:])], 1)
        last, back, total = lax.optimization_barrier((last, back, add(SECOND, later, total)))
        total = add(THIRD, last, add(LENT, back, total))
    else:
        total = add(HEAD, gathered, total)

    if lax.axis_size("row") == 2 and lax.axis_size("col") == 4:
        ladder = reduce_plane(z, total)
    else:
        ladder = lax.psum_scatter(total, ("row", "col"), scatter_dimension=0, tiled=True)
    out_pairs = ladder.shape[0]
    local_a = WIN // groups
    grid = ladder.reshape(out_pairs, local_a, groups, local_a)
    received = lax.all_to_all(grid, "pair", split_axis=2, concat_axis=2, tiled=True)
    swapped = jnp.transpose(received, (0, 3, 2, 1)).reshape(out_pairs, local_a * WIN)
    return (0.5 * (ladder - swapped)).astype(jnp.bfloat16)


def solution(mesh):
    return jax.shard_map(
        per_device,
        mesh=mesh,
        in_specs=(P("pair", "row", "col"), P("pair", "row", "col"), P(), P()),
        out_specs=P(("row", "col"), "pair"),
        check_vma=False,
    )
```

```python
import functools

import jax
import jax.numpy as jnp
from jax import lax
from jax.experimental import pallas as pl
from jax.experimental.pallas import tpu as pltpu
from jax.sharding import PartitionSpec as P

TILE = 64
WIN = 64
LANES = 128
AB_BLOCK = 512
PIECE = 4
VMEM_LIMIT = 50 * 1024 * 1024

LAST, LONG, CORE, LENT, UNITS = 0, 1, 2, 3, 8
HEAD, SECOND, THIRD, RARE = 0, 1, 2, 3


class Sizes:
    def __init__(self, amps, integrals):
        self.pairs, self.local_c, self.local_d = amps.shape
        self.local_ab = integrals.shape[0]
        self.uc = min(self.local_c, TILE)
        self.ud = min(self.local_d, TILE)
        self.nud = self.local_d // self.ud
        self.units = (self.local_c // self.uc) * self.nud
        self.half = self.pairs // 2
        self.rows = self.uc // 2
        self.k = self.rows * LANES
        self.most = 2 * self.units
        self.long = self.most > PIECE
        self.places = (4 if self.long else 1) * PIECE
        self.slot_mine = UNITS + self.units
        self.slot_other = self.slot_mine + self.places
        self.table = self.slot_other + self.places


def lending(counts, here, there):
    move = jnp.minimum((here - there) // 2, 2)
    richer = jnp.where(counts[0] >= counts[1], 0, 1)
    return [jnp.where((counts[c] > 0) & ((move == 2) | ((move == 1) & (richer == c))), 1, 0) for c in range(2)]


def plan_kernel(z, rows, cols, pos_ref, ma_ref, mi_ref, table_ref):
    row, col = pos_ref[0], pos_ref[1]
    core, chip = lax.rem(col, 2), col // 2

    def active(r, c, unit):
        ct = (r * z.local_c + (unit // z.nud) * z.uc) // TILE
        dt = (c * z.local_d + lax.rem(unit, z.nud) * z.ud) // TILE
        return jnp.where(ma_ref[ct, dt] * mi_ref[ct, dt] != 0, 1, 0)

    def count(r, c):
        return lax.fori_loop(0, z.units, lambda u, n: n + active(r, c, u), 0)

    table_ref[CORE] = core
    for i in range(z.units):
        table_ref[UNITS + i] = 0

    def fill(u, n):
        on = active(row, col, u)

        @pl.when(on == 1)
        def _():
            table_ref[UNITS + n] = u

        return n + on

    own = lax.fori_loop(0, z.units, fill, 0)
    zero = jnp.int32(0)
    if z.long:
        grid = [(r, x) for r in range(2) for x in range(2)]
        n = {g: [count(g[0], 2 * g[1] + c) for c in range(2)] for g in grid}
        all_n = {g: n[g][0] + n[g][1] for g in grid}
        lent_x = {(r, x): lending(n[r, x], all_n[r, x], all_n[r, 1 - x]) for r, x in grid}
        n = {g: [n[g][c] - lent_x[g][c] for c in range(2)] for g in grid}
        all_n = {(r, x): sum(n[r, x]) + sum(lent_x[r, 1 - x]) for r, x in grid}
        lent_y = {(r, x): lending(n[r, x], all_n[r, x], all_n[1 - r, x]) for r, x in grid}
        n = {g: [n[g][c] - lent_y[g][c] for c in range(2)] for g in grid}
        all_n = {(r, x): sum(n[r, x]) + sum(lent_x[r, 1 - x]) + sum(lent_y[1 - r, x]) for r, x in grid}
        slots = jnp.int32(1)
        for g in grid:
            slots = jnp.maximum(slots, all_n[g])

        def here(get):
            upper = jnp.where(chip == 0, get(0, 0), get(0, 1))
            return jnp.where(row == 0, upper, jnp.where(chip == 0, get(1, 0), get(1, 1)))

        kept = [here(lambda r, x: n[r, x][c]) for c in range(2)]
        gives = [here(lambda r, x: jnp.where(core == 0, v[r, x][0], v[r, x][1])) for v in (lent_x, lent_y)]
        got = [here(lambda r, x: lent_x[r, 1 - x][c]) for c in range(2)]
        got += [here(lambda r, x: lent_y[1 - r, x][c]) for c in range(2)]
        is_long = slots > 3 * PIECE
        last_len = jnp.maximum(slots - jnp.where(is_long, 3, 2) * PIECE, 0)
    else:

        def most(g, n):
            r, x = g // (cols // 2), lax.rem(g, cols // 2)
            return jnp.maximum(n, count(r, 2 * x) + count(r, 2 * x + 1))

        slots = lax.fori_loop(0, rows * (cols // 2), most, 1)
        other = count(row, col + 1 - 2 * core)
        kept = [jnp.where(core == 0, own, other), jnp.where(core == 0, other, own)]
        gives, got = [zero, zero], [zero] * 4
        is_long, last_len = slots > PIECE, slots
    table_ref[LAST] = last_len
    table_ref[LONG] = jnp.where(is_long, 1, 0)
    for d in range(2):
        at = own - 1 - (gives[0] if d else 0)
        table_ref[LENT + d] = jnp.where(gives[d] == 1, table_ref[UNITS + jnp.clip(at, 0, z.units - 1)], -1)

    first, second = kept
    extra = jnp.abs(first - second)
    richer = jnp.where(first >= second, 0, 1)
    for at in range(z.places):
        piece, j = divmod(at, PIECE)
        borrowed = jnp.bool_(False)
        s = zero + at
        if piece == SECOND:
            borrowed = got[j] == 1
            s = s - sum(got[:j], zero)
        elif piece == THIRD:
            s = s - sum(got, zero) + jnp.where(is_long, PIECE, 0)
        elif piece == RARE:
            s = s - sum(got, zero) - PIECE
        live = jnp.logical_not(borrowed) & (s < first + second)
        if piece == RARE:
            live &= is_long
        k = s - extra
        owner = jnp.where(s < extra, richer, lax.rem(jnp.maximum(k, 0), 2))
        index = jnp.where(s < extra, s, k // 2 + jnp.where(owner == richer, extra, 0))
        unit = table_ref[UNITS + jnp.clip(index, 0, z.units - 1)]
        mine = jnp.where(live & (owner == core), unit, -1)
        theirs = live & (owner != core)
        if piece == SECOND:
            mine = jnp.where(borrowed & (core == j % 2), z.units + j // 2, mine)
            theirs |= borrowed & (core != j % 2)
        table_ref[z.slot_mine + at] = mine
        table_ref[z.slot_other + at] = jnp.where(theirs, 1, 0)


def make_plan(z, mask_amps, mask_ints):
    rows, cols = lax.axis_size("row"), lax.axis_size("col")
    pos = jnp.stack([lax.axis_index("row"), lax.axis_index("col")]).astype(jnp.int32)
    smem = pl.BlockSpec(memory_space=pltpu.SMEM)
    return pl.pallas_call(
        functools.partial(plan_kernel, z, rows, cols),
        out_shape=jax.ShapeDtypeStruct((z.table,), jnp.int32),
        in_specs=[smem] * 3,
        out_specs=smem,
        name="plan",
    )(pos, mask_amps, mask_ints)


def squeeze_tile(second, x, y):
    low = lax.broadcasted_iota(jnp.int32, x.shape, 2) < TILE
    if second:
        return jnp.where(low, jnp.concatenate([x[..., TILE:], x[..., :TILE]], -1), y)
    return jnp.where(low, x, jnp.concatenate([y[..., TILE:], y[..., :TILE]], -1))


def pack_tile(z, unit, on, a_ref, o_ref):
    for second in range(z.nud):

        @pl.when(on & (lax.rem(unit, z.nud) == second))
        def _(second=second):
            v = squeeze_tile(second, a_ref[:, : z.rows, :], a_ref[:, z.rows :, :])
            o_ref[0] = v.reshape(z.half, z.k)


def pack_slots(z, table, amps, start, count, kept, borrowed=(), received=None):
    def unit_of(t, i):
        return t[z.slot_mine + start + i]

    def other(t, i):
        return t[z.slot_other + start + i]

    def half(t):
        return t[CORE] if kept else 1 - t[CORE]

    def tile(t, i):
        unit = unit_of(t, i)
        return jnp.where((unit >= 0) & (unit < z.units), unit, 0) // z.nud

    def body(t, a_ref, *refs):
        o_ref = refs[-1]
        i = pl.program_id(0)
        unit = unit_of(t, i)
        pack_tile(z, unit, (unit >= 0) & (unit < z.units), a_ref, o_ref)
        for d in range(len(borrowed)):

            @pl.when(unit == z.units + d)
            def _(d=d):
                o_ref[0] = refs[d][0]

        if kept:

            @pl.when(other(t, i) == 1)
            def _():
                o_ref[0] = refs[-2][0]

    in_specs = [pl.BlockSpec((z.half, z.uc, LANES), lambda i, t: (half(t), tile(t, i), 0))]
    in_specs += [pl.BlockSpec((1, z.half, z.k), lambda i, t: (half(t), 0, 0))] * len(borrowed)
    args = [amps, *borrowed]
    if kept:
        in_specs.append(pl.BlockSpec((1, z.half, z.k), lambda i, t: (jnp.where(other(t, i) == 1, i, 0), 0, 0)))
        args.append(received)
    return pl.pallas_call(
        body,
        grid_spec=pltpu.PrefetchScalarGridSpec(
            num_scalar_prefetch=1,
            grid=(count,),
            in_specs=in_specs,
            out_specs=pl.BlockSpec((1, z.half, z.k), lambda i, t: (i, 0, 0)),
        ),
        out_shape=jax.ShapeDtypeStruct((count, z.half, z.k), jnp.bfloat16),
        compiler_params=pltpu.CompilerParams(vmem_limit_bytes=VMEM_LIMIT),
        cost_estimate=pl.CostEstimate(flops=0, bytes_accessed=4 * count * z.half * z.k * 2, transcendentals=0),
        name="pack_kept" if kept else "pack_given",
    )(table, *args)


def lend_amps(z, table, amps, way):
    def body(t, a_ref, o_ref):
        unit = t[LENT + way]
        pack_tile(z, unit, unit >= 0, a_ref, o_ref)

    return pl.pallas_call(
        body,
        grid_spec=pltpu.PrefetchScalarGridSpec(
            num_scalar_prefetch=1,
            grid=(2,),
            in_specs=[
                pl.BlockSpec((z.half, z.uc, LANES), lambda h, t: (h, jnp.maximum(t[LENT + way], 0) // z.nud, 0))
            ],
            out_specs=pl.BlockSpec((1, z.half, z.k), lambda h, t: (h, 0, 0)),
        ),
        out_shape=jax.ShapeDtypeStruct((2, z.half, z.k), jnp.bfloat16),
        compiler_params=pltpu.CompilerParams(vmem_limit_bytes=VMEM_LIMIT),
        name="lend_amps",
    )(table, amps)


def lend_integrals(z, table, integrals, way, part):
    ab = AB_BLOCK // 2
    steps = z.local_ab // 2 // ab

    def body(t, x_ref, y_ref, o_ref):
        unit = t[LENT + way]
        for second in range(z.nud):

            @pl.when((unit >= 0) & (lax.rem(unit, z.nud) == second))
            def _(second=second):
                o_ref[...] = squeeze_tile(second, x_ref[...], y_ref[...])

    def imap(offset):
        return lambda j, t: (part * steps + j, jnp.maximum(t[LENT + way], 0) // z.nud * 2 + offset, 0)

    return pl.pallas_call(
        body,
        grid_spec=pltpu.PrefetchScalarGridSpec(
            num_scalar_prefetch=1,
            grid=(steps,),
            in_specs=[pl.BlockSpec((ab, z.rows, LANES), imap(0)), pl.BlockSpec((ab, z.rows, LANES), imap(1))],
            out_specs=pl.BlockSpec((ab, z.rows, LANES), lambda j, t: (j, 0, 0)),
        ),
        out_shape=jax.ShapeDtypeStruct((z.local_ab // 2, z.rows, LANES), jnp.bfloat16),
        compiler_params=pltpu.CompilerParams(vmem_limit_bytes=VMEM_LIMIT),
        name="lend_integrals",
    )(table, integrals, integrals)


def pack(z, table, amps, piece, borrowed=()):
    start = piece * PIECE
    given = swap_cores(pack_slots(z, table, amps, start, PIECE, False, borrowed))
    return pack_slots(z, table, amps, start, PIECE, True, borrowed, given)


def ladder_piece(z, table, piece, gathered, integrals, total, borrowed=()):
    groups, count = gathered.shape[:2]
    swapped = swap_cores(gathered)
    ab = min(AB_BLOCK // 2 if borrowed else AB_BLOCK, z.local_ab)
    step = min(z.rows, 16)
    per_unit = z.uc // z.rows
    split = z.rows % 16 == 0

    def unit_of(t, s):
        return t[z.slot_mine + piece * PIECE + s]

    def tile(t, s):
        unit = unit_of(t, s)
        return jnp.where((unit >= 0) & (unit < z.units), unit, 0) // z.nud

    def body(t, g_ref, w_ref, prev_ref, *rest):
        lent_refs, rest = rest[: len(borrowed)], rest[len(borrowed) :]
        if split:
            x_ref, y_ref, out_ref, a_ref, b_ref = rest
        else:
            x_ref, out_ref, a_ref, b_ref = rest
        s = pl.program_id(1)
        core = t[CORE]
        unit = unit_of(t, s)

        @pl.when(s == 0)
        def _():
            out_ref[...] = prev_ref[...]

        @pl.when(unit >= 0)
        def _():
            for g in range(groups):
                here = pl.multiple_of(g * z.pairs + core * z.half, z.half)
                there = pl.multiple_of(g * z.pairs + (1 - core) * z.half, z.half)
                a_ref[pl.ds(here, z.half)] = g_ref[g, 0]
                a_ref[pl.ds(there, z.half)] = w_ref[g, 0]

        for second in range(z.nud):

            @pl.when((unit >= 0) & (unit < z.units) & (lax.rem(unit, z.nud) == second))
            def _(second=second):
                for k in range(z.rows // step):
                    at = slice(k * step, (k + 1) * step)
                    up = slice(z.rows + k * step, z.rows + (k + 1) * step)
                    x, y = (x_ref[:, at], y_ref[:, at]) if split else (x_ref[:, at], x_ref[:, up])
                    b_ref[:, k * step * LANES : (k + 1) * step * LANES] = squeeze_tile(second, x, y).reshape(
                        ab, step * LANES
                    )

        for d in range(len(borrowed)):
            upper = pl.program_id(0) >= parts // 2

            @pl.when((unit == z.units + d // 2) & (upper == (d % 2 == 1)))
            def _(d=d):
                for k in range(z.rows // step):
                    b_ref[:, k * step * LANES : (k + 1) * step * LANES] = lent_refs[d][
                        :, k * step : (k + 1) * step
                    ].reshape(ab, step * LANES)

        @pl.when(unit >= 0)
        def _():
            def add(k, _):
                cols = pl.ds(pl.multiple_of(k * step * LANES, step * LANES), step * LANES)
                out_ref[...] += lax.dot_general(
                    a_ref[:, cols], b_ref[:, cols], (((1,), (1,)), ((), ())), preferred_element_type=jnp.float32
                )
                return 0

            lax.fori_loop(0, z.rows // step, add, 0)

    def imap(offset):
        def index(j, s, t):
            return (j, tile(t, s) * per_unit + offset, 0)

        return index

    piece_spec = pl.BlockSpec((groups, 1, z.half, z.k), lambda j, s, t: (0, s, 0, 0))
    out_spec = pl.BlockSpec((groups * z.pairs, ab), lambda j, s, t: (0, j))
    if split:
        ints_specs = [pl.BlockSpec((ab, z.rows, LANES), imap(0)), pl.BlockSpec((ab, z.rows, LANES), imap(1))]
        ints = [integrals, integrals]
    else:
        ints_specs = [pl.BlockSpec((ab, z.uc, LANES), lambda j, s, t: (j, tile(t, s), 0))]
        ints = [integrals]
    parts = z.local_ab // ab
    lower_spec = pl.BlockSpec((ab, z.rows, LANES), lambda j, s, t: (jnp.minimum(j, parts // 2 - 1), 0, 0))
    upper_spec = pl.BlockSpec((ab, z.rows, LANES), lambda j, s, t: (jnp.maximum(j - parts // 2, 0), 0, 0))
    lent_specs = [lower_spec, upper_spec] * (len(borrowed) // 2)
    return pl.pallas_call(
        body,
        grid_spec=pltpu.PrefetchScalarGridSpec(
            num_scalar_prefetch=1,
            grid=(z.local_ab // ab, count),
            in_specs=[piece_spec, piece_spec, out_spec] + lent_specs + ints_specs,
            out_specs=out_spec,
            scratch_shapes=[
                pltpu.VMEM((groups * z.pairs, z.k), jnp.bfloat16),
                pltpu.VMEM((ab, z.k), jnp.bfloat16),
            ],
        ),
        out_shape=jax.ShapeDtypeStruct((groups * z.pairs, z.local_ab), jnp.float32),
        input_output_aliases={3: 0},
        compiler_params=pltpu.CompilerParams(vmem_limit_bytes=VMEM_LIMIT),
        cost_estimate=pl.CostEstimate(
            flops=2 * groups * z.pairs * z.local_ab * z.k * count,
            bytes_accessed=2 * z.local_ab * z.uc * LANES * count,
            transcendentals=0,
        ),
        name="ladder_piece",
    )(table, gathered, swapped, total, *borrowed, *ints)


def swap_cores(x):
    return lax.ppermute(x, "col", [(i, i ^ 1) for i in range(lax.axis_size("col"))])


def over_row(x):
    return lax.ppermute(x, "row", [(0, 1), (1, 0)])


def over_chip(x):
    return lax.ppermute(x, "col", [(i, i ^ 2) for i in range(4)])


def pick(x, at, axis):
    return lax.dynamic_index_in_dim(x, at, axis, keepdims=False)


def reduce_plane(z, total):
    row, col = lax.axis_index("row"), lax.axis_index("col")
    chip, core = col // 2, lax.rem(col, 2)

    def halve(x, at, axis, send):
        return pick(x, at, axis) + send(pick(x, 1 - at, axis))

    wide = z.local_ab // 2
    rest = total.reshape(2, 2, 2, z.half, z.local_ab)
    rest = halve(rest, core, 2, swap_cores)
    left, right = rest[..., :wide], rest[..., wide:]
    left = halve(left, row, 0, over_row)
    right = halve(right, chip, 1, over_chip)
    left = halve(left, chip, 0, over_chip)
    right = halve(right, row, 0, over_row)
    return jnp.concatenate([left, right], -1)


def per_device(amps, integrals, mask_amps, mask_ints):
    z = Sizes(amps, integrals)
    table = make_plan(z, mask_amps, mask_ints)
    groups = lax.axis_size("pair")

    def gather(own):
        return lax.all_gather(own, "pair")

    def add(piece, gathered, total, borrowed=()):
        return ladder_piece(z, table, piece, gathered, integrals, total, borrowed)

    def rare(total):
        return add(RARE, gather(pack(z, table, amps, RARE)), total)

    def finish(count, piece, own, second, total, borrowed):
        if count:
            last = gather(own[:count])
        if second is not None:
            total = add(SECOND, second, total, borrowed)
        if count:
            last, total = lax.optimization_barrier((last, total))
            total = add(piece, last, total)
        return total

    total = jnp.zeros((groups * z.pairs, z.local_ab), jnp.float32)
    head = pack(z, table, amps, HEAD)
    if z.long:
        first = gather(head)
        lent = over_chip(lend_amps(z, table, amps, 0)), over_row(lend_amps(z, table, amps, 1))
        ints = [[lend_integrals(z, table, integrals, way, part) for way in range(2)] for part in range(2)]
        lent, ints = lax.optimization_barrier((lent, ints))
        own = pack(z, table, amps, SECOND, lent)
        lower = over_chip(ints[0][0]), over_row(ints[0][1])
        third = pack(z, table, amps, THIRD)
        first, own, lower, third, rest = lax.optimization_barrier((first, own, lower, third, ints[1]))
        second = gather(own)
        upper = over_chip(rest[0]), over_row(rest[1])
        second, upper, total = lax.optimization_barrier((second, upper, add(HEAD, first, total)))
        borrowed = lower[0], upper[0], lower[1], upper[1]
        total = lax.cond(table[LONG] == 1, rare, lambda t: t, total)
        ends = [functools.partial(finish, n, THIRD) for n in range(PIECE + 1)]
        total = lax.switch(table[LAST], ends, third, second, total, borrowed)
    else:
        ends = [functools.partial(finish, n, HEAD) for n in range(1, PIECE + 1)]
        total = lax.switch(table[LAST] - 1, ends, head, None, total, ())

    if lax.axis_size("row") == 2 and lax.axis_size("col") == 4:
        ladder = lax.optimization_barrier(reduce_plane(z, total))
    else:
        ladder = lax.psum_scatter(total, ("row", "col"), scatter_dimension=0, tiled=True)
    out_pairs = ladder.shape[0]
    local_a = WIN // groups
    grid = ladder.reshape(out_pairs, local_a, groups, local_a)
    received = lax.all_to_all(grid, "pair", split_axis=2, concat_axis=2, tiled=True)
    swapped = jnp.transpose(received, (0, 3, 2, 1)).reshape(out_pairs, local_a * WIN)
    return (0.5 * (ladder - swapped)).astype(jnp.bfloat16)


def solution(mesh):
    return jax.shard_map(
        per_device,
        mesh=mesh,
        in_specs=(P("pair", "row", "col"), P("pair", "row", "col"), P(), P()),
        out_specs=P(("row", "col"), "pair"),
        check_vma=False,
    )
```

```python
import functools

import jax
import jax.numpy as jnp
from jax import lax
from jax.experimental import pallas as pl
from jax.experimental.pallas import tpu as pltpu
from jax.sharding import PartitionSpec as P

TILE = 64
WIN = 64
LANES = 128
AB_BLOCK = 512
PIECE = 4
VMEM_LIMIT = 50 * 1024 * 1024

LAST, LONG, CORE, LENT, UNITS = 0, 1, 2, 3, 8
HEAD, SECOND, THIRD, RARE = 0, 1, 2, 3


class Sizes:
    def __init__(self, amps, integrals):
        self.pairs, self.local_c, self.local_d = amps.shape
        self.local_ab = integrals.shape[0]
        self.uc = min(self.local_c, TILE)
        self.ud = min(self.local_d, TILE)
        self.nud = self.local_d // self.ud
        self.units = (self.local_c // self.uc) * self.nud
        self.half = self.pairs // 2
        self.rows = self.uc // 2
        self.k = self.rows * LANES
        self.most = 2 * self.units
        self.long = self.most > PIECE
        self.places = (4 if self.long else 1) * PIECE
        self.slot_mine = UNITS + self.units
        self.slot_other = self.slot_mine + self.places
        self.table = self.slot_other + self.places


def lending(counts, here, there):
    move = jnp.minimum((here - there) // 2, 2)
    richer = jnp.where(counts[0] >= counts[1], 0, 1)
    return [jnp.where((counts[c] > 0) & ((move == 2) | ((move == 1) & (richer == c))), 1, 0) for c in range(2)]


def plan_kernel(z, rows, cols, pos_ref, ma_ref, mi_ref, table_ref):
    row, col = pos_ref[0], pos_ref[1]
    core, chip = lax.rem(col, 2), col // 2

    def active(r, c, unit):
        ct = (r * z.local_c + (unit // z.nud) * z.uc) // TILE
        dt = (c * z.local_d + lax.rem(unit, z.nud) * z.ud) // TILE
        return jnp.where(ma_ref[ct, dt] * mi_ref[ct, dt] != 0, 1, 0)

    def count(r, c):
        return lax.fori_loop(0, z.units, lambda u, n: n + active(r, c, u), 0)

    table_ref[CORE] = core
    for i in range(z.units):
        table_ref[UNITS + i] = 0

    def fill(u, n):
        on = active(row, col, u)

        @pl.when(on == 1)
        def _():
            table_ref[UNITS + n] = u

        return n + on

    own = lax.fori_loop(0, z.units, fill, 0)
    zero = jnp.int32(0)
    if z.long:
        grid = [(r, x) for r in range(2) for x in range(2)]
        n = {g: [count(g[0], 2 * g[1] + c) for c in range(2)] for g in grid}
        all_n = {g: n[g][0] + n[g][1] for g in grid}
        lent_x = {(r, x): lending(n[r, x], all_n[r, x], all_n[r, 1 - x]) for r, x in grid}
        n = {g: [n[g][c] - lent_x[g][c] for c in range(2)] for g in grid}
        all_n = {(r, x): sum(n[r, x]) + sum(lent_x[r, 1 - x]) for r, x in grid}
        lent_y = {(r, x): lending(n[r, x], all_n[r, x], all_n[1 - r, x]) for r, x in grid}
        n = {g: [n[g][c] - lent_y[g][c] for c in range(2)] for g in grid}
        all_n = {(r, x): sum(n[r, x]) + sum(lent_x[r, 1 - x]) + sum(lent_y[1 - r, x]) for r, x in grid}
        slots = jnp.int32(1)
        for g in grid:
            slots = jnp.maximum(slots, all_n[g])

        def here(get):
            upper = jnp.where(chip == 0, get(0, 0), get(0, 1))
            return jnp.where(row == 0, upper, jnp.where(chip == 0, get(1, 0), get(1, 1)))

        kept = [here(lambda r, x: n[r, x][c]) for c in range(2)]
        gives = [here(lambda r, x: jnp.where(core == 0, v[r, x][0], v[r, x][1])) for v in (lent_x, lent_y)]
        got = [here(lambda r, x: lent_x[r, 1 - x][c]) for c in range(2)]
        got += [here(lambda r, x: lent_y[1 - r, x][c]) for c in range(2)]
        is_long = slots > 3 * PIECE
        last_len = jnp.maximum(slots - jnp.where(is_long, 3, 2) * PIECE, 0)
    else:

        def most(g, n):
            r, x = g // (cols // 2), lax.rem(g, cols // 2)
            return jnp.maximum(n, count(r, 2 * x) + count(r, 2 * x + 1))

        slots = lax.fori_loop(0, rows * (cols // 2), most, 1)
        other = count(row, col + 1 - 2 * core)
        kept = [jnp.where(core == 0, own, other), jnp.where(core == 0, other, own)]
        gives, got = [zero, zero], [zero] * 4
        is_long, last_len = slots > PIECE, slots
    table_ref[LAST] = last_len
    table_ref[LONG] = jnp.where(is_long, 1, 0)
    for d in range(2):
        at = own - 1 - (gives[0] if d else 0)
        table_ref[LENT + d] = jnp.where(gives[d] == 1, table_ref[UNITS + jnp.clip(at, 0, z.units - 1)], -1)

    first, second = kept
    extra = jnp.abs(first - second)
    richer = jnp.where(first >= second, 0, 1)
    for at in range(z.places):
        piece, j = divmod(at, PIECE)
        borrowed = jnp.bool_(False)
        s = zero + at
        if piece == SECOND:
            borrowed = got[j] == 1
            s = s - sum(got[:j], zero)
        elif piece == THIRD:
            s = s - sum(got, zero) + jnp.where(is_long, PIECE, 0)
        elif piece == RARE:
            s = s - sum(got, zero) - PIECE
        live = jnp.logical_not(borrowed) & (s < first + second)
        if piece == RARE:
            live &= is_long
        k = s - extra
        owner = jnp.where(s < extra, richer, lax.rem(jnp.maximum(k, 0), 2))
        index = jnp.where(s < extra, s, k // 2 + jnp.where(owner == richer, extra, 0))
        unit = table_ref[UNITS + jnp.clip(index, 0, z.units - 1)]
        mine = jnp.where(live & (owner == core), unit, -1)
        theirs = live & (owner != core)
        if piece == SECOND:
            mine = jnp.where(borrowed & (core == j % 2), z.units + j // 2, mine)
            theirs |= borrowed & (core != j % 2)
        table_ref[z.slot_mine + at] = mine
        table_ref[z.slot_other + at] = jnp.where(theirs, 1, 0)


def make_plan(z, mask_amps, mask_ints):
    rows, cols = lax.axis_size("row"), lax.axis_size("col")
    pos = jnp.stack([lax.axis_index("row"), lax.axis_index("col")]).astype(jnp.int32)
    smem = pl.BlockSpec(memory_space=pltpu.SMEM)
    return pl.pallas_call(
        functools.partial(plan_kernel, z, rows, cols),
        out_shape=jax.ShapeDtypeStruct((z.table,), jnp.int32),
        in_specs=[smem] * 3,
        out_specs=smem,
        name="plan",
    )(pos, mask_amps, mask_ints)


def squeeze_tile(second, x, y):
    low = lax.broadcasted_iota(jnp.int32, x.shape, 2) < TILE
    if second:
        return jnp.where(low, jnp.concatenate([x[..., TILE:], x[..., :TILE]], -1), y)
    return jnp.where(low, x, jnp.concatenate([y[..., TILE:], y[..., :TILE]], -1))


def pack_tile(z, unit, on, a_ref, o_ref):
    for second in range(z.nud):

        @pl.when(on & (lax.rem(unit, z.nud) == second))
        def _(second=second):
            v = squeeze_tile(second, a_ref[:, : z.rows, :], a_ref[:, z.rows :, :])
            o_ref[0] = v.reshape(z.half, z.k)


def pack_slots(z, table, amps, start, count, kept, borrowed=(), received=None):
    def unit_of(t, i):
        return t[z.slot_mine + start + i]

    def other(t, i):
        return t[z.slot_other + start + i]

    def half(t):
        return t[CORE] if kept else 1 - t[CORE]

    def tile(t, i):
        unit = unit_of(t, i)
        return jnp.where((unit >= 0) & (unit < z.units), unit, 0) // z.nud

    def body(t, a_ref, *refs):
        o_ref = refs[-1]
        i = pl.program_id(0)
        unit = unit_of(t, i)
        pack_tile(z, unit, (unit >= 0) & (unit < z.units), a_ref, o_ref)
        for d in range(len(borrowed)):

            @pl.when(unit == z.units + d)
            def _(d=d):
                o_ref[0] = refs[d][0]

        if kept:

            @pl.when(other(t, i) == 1)
            def _():
                o_ref[0] = refs[-2][0]

    in_specs = [pl.BlockSpec((z.half, z.uc, LANES), lambda i, t: (half(t), tile(t, i), 0))]
    in_specs += [pl.BlockSpec((1, z.half, z.k), lambda i, t: (half(t), 0, 0))] * len(borrowed)
    args = [amps, *borrowed]
    if kept:
        in_specs.append(pl.BlockSpec((1, z.half, z.k), lambda i, t: (jnp.where(other(t, i) == 1, i, 0), 0, 0)))
        args.append(received)
    return pl.pallas_call(
        body,
        grid_spec=pltpu.PrefetchScalarGridSpec(
            num_scalar_prefetch=1,
            grid=(count,),
            in_specs=in_specs,
            out_specs=pl.BlockSpec((1, z.half, z.k), lambda i, t: (i, 0, 0)),
        ),
        out_shape=jax.ShapeDtypeStruct((count, z.half, z.k), jnp.bfloat16),
        compiler_params=pltpu.CompilerParams(vmem_limit_bytes=VMEM_LIMIT),
        cost_estimate=pl.CostEstimate(flops=0, bytes_accessed=4 * count * z.half * z.k * 2, transcendentals=0),
        name="pack_kept" if kept else "pack_given",
    )(table, *args)


def lend_amps(z, table, amps, way):
    def body(t, a_ref, o_ref):
        unit = t[LENT + way]
        pack_tile(z, unit, unit >= 0, a_ref, o_ref)

    return pl.pallas_call(
        body,
        grid_spec=pltpu.PrefetchScalarGridSpec(
            num_scalar_prefetch=1,
            grid=(2,),
            in_specs=[
                pl.BlockSpec((z.half, z.uc, LANES), lambda h, t: (h, jnp.maximum(t[LENT + way], 0) // z.nud, 0))
            ],
            out_specs=pl.BlockSpec((1, z.half, z.k), lambda h, t: (h, 0, 0)),
        ),
        out_shape=jax.ShapeDtypeStruct((2, z.half, z.k), jnp.bfloat16),
        compiler_params=pltpu.CompilerParams(vmem_limit_bytes=VMEM_LIMIT),
        name="lend_amps",
    )(table, amps)


def lend_integrals(z, table, integrals, way, part):
    ab = AB_BLOCK // 2
    steps = z.local_ab // 2 // ab

    def body(t, x_ref, y_ref, o_ref):
        unit = t[LENT + way]
        for second in range(z.nud):

            @pl.when((unit >= 0) & (lax.rem(unit, z.nud) == second))
            def _(second=second):
                def relay(i):
                    at = pl.ds(i * 32, 32)
                    o_ref[at] = squeeze_tile(second, x_ref[at], y_ref[at])

                each(ab // 32, relay)

    def imap(offset):
        return lambda j, t: (part * steps + j, jnp.maximum(t[LENT + way], 0) // z.nud * 2 + offset, 0)

    return pl.pallas_call(
        body,
        grid_spec=pltpu.PrefetchScalarGridSpec(
            num_scalar_prefetch=1,
            grid=(steps,),
            in_specs=[pl.BlockSpec((ab, z.rows, LANES), imap(0)), pl.BlockSpec((ab, z.rows, LANES), imap(1))],
            out_specs=pl.BlockSpec((ab, z.rows, LANES), lambda j, t: (j, 0, 0)),
        ),
        out_shape=jax.ShapeDtypeStruct((z.local_ab // 2, z.rows, LANES), jnp.bfloat16),
        compiler_params=pltpu.CompilerParams(vmem_limit_bytes=VMEM_LIMIT),
        name="lend_integrals",
    )(table, integrals, integrals)


def pack(z, table, amps, piece, borrowed=()):
    start = piece * PIECE
    given = swap_cores(pack_slots(z, table, amps, start, PIECE, False, borrowed))
    return pack_slots(z, table, amps, start, PIECE, True, borrowed, given)


def each(count, body):
    def step(i, carry):
        body(i)
        return carry

    lax.fori_loop(0, count, step, 0)


def ladder_piece(z, table, piece, gathered, integrals, total, borrowed=()):
    groups, count = gathered.shape[:2]
    swapped = swap_cores(gathered)
    ab = min(AB_BLOCK // 2 if borrowed else AB_BLOCK, z.local_ab)
    parts = z.local_ab // ab
    few, many, deep = 64, 256, min(z.k, 1024)
    per_unit = z.uc // z.rows
    split = z.rows % 16 == 0
    m = groups * z.half

    def by_lines(x):
        return x.reshape(-1, few, *x.shape[1:])

    def unit_of(t, s):
        return t[z.slot_mine + piece * PIECE + s]

    def tile(t, s):
        unit = unit_of(t, s)
        return jnp.where((unit >= 0) & (unit < z.units), unit, 0) // z.nud

    def body(t, g_ref, w_ref, prev_ref, *rest):
        lent_refs, rest = rest[: len(borrowed)], rest[len(borrowed) :]
        if split:
            x_ref, y_ref, out_ref, b_ref = rest
        else:
            x_ref, out_ref, b_ref = rest
        s = pl.program_id(1)
        unit = unit_of(t, s)

        @pl.when(s == 0)
        def _():
            out_ref[...] = prev_ref[...]

        for second in range(z.nud):

            @pl.when((unit >= 0) & (unit < z.units) & (lax.rem(unit, z.nud) == second))
            def _(second=second):
                def relay(i):
                    if split:
                        x, y = x_ref[i], y_ref[i]
                    else:
                        x, y = x_ref[i, :, : z.rows], x_ref[i, :, z.rows :]
                    b_ref[i] = squeeze_tile(second, x, y).reshape(few, z.k)

                each(ab // few, relay)

        for d in range(len(borrowed)):
            upper = pl.program_id(0) >= parts // 2

            @pl.when((unit == z.units + d // 2) & (upper == (d % 2 == 1)))
            def _(d=d):
                def relay(i):
                    b_ref[i] = lent_refs[d][i].reshape(few, z.k)

                each(ab // few, relay)

        @pl.when(unit >= 0)
        def _():
            def product(i):
                n, k = i // (z.k // deep), lax.rem(i, z.k // deep)
                at = pl.ds(pl.multiple_of(n * many, many), many)
                cols = pl.ds(pl.multiple_of(k * deep, deep), deep)
                b = b_ref[pl.ds(n * (many // few), many // few), :, cols].reshape(many, deep)
                for h, a_ref in enumerate((g_ref, w_ref)):
                    out_ref[h * m : (h + 1) * m, at] += lax.dot_general(
                        a_ref[:, 0, :, cols].reshape(m, deep),
                        b,
                        (((1,), (1,)), ((), ())),
                        preferred_element_type=jnp.float32,
                    )

            each((ab // many) * (z.k // deep), product)

    def imap(offset):
        def index(j, s, t):
            return (j, 0, tile(t, s) * per_unit + offset, 0)

        return index

    piece_spec = pl.BlockSpec((groups, 1, z.half, z.k), lambda j, s, t: (0, s, 0, 0))
    out_spec = pl.BlockSpec((groups * z.pairs, ab), lambda j, s, t: (0, j))
    if split:
        ints_specs = [pl.BlockSpec((ab // few, few, z.rows, LANES), imap(offset)) for offset in range(2)]
        ints = [by_lines(integrals)] * 2
    else:
        ints_specs = [pl.BlockSpec((ab // few, few, z.uc, LANES), lambda j, s, t: (j, 0, tile(t, s), 0))]
        ints = [by_lines(integrals)]
    low_spec = pl.BlockSpec((ab // few, few, z.rows, LANES), lambda j, s, t: (jnp.minimum(j, parts // 2 - 1), 0, 0, 0))
    high_spec = pl.BlockSpec((ab // few, few, z.rows, LANES), lambda j, s, t: (jnp.maximum(j - parts // 2, 0), 0, 0, 0))
    lent_specs = [low_spec, high_spec] * (len(borrowed) // 2)
    return pl.pallas_call(
        body,
        grid_spec=pltpu.PrefetchScalarGridSpec(
            num_scalar_prefetch=1,
            grid=(z.local_ab // ab, count),
            in_specs=[piece_spec, piece_spec, out_spec] + lent_specs + ints_specs,
            out_specs=out_spec,
            scratch_shapes=[pltpu.VMEM((ab // few, few, z.k), jnp.bfloat16)],
        ),
        out_shape=jax.ShapeDtypeStruct((groups * z.pairs, z.local_ab), jnp.float32),
        input_output_aliases={3: 0},
        compiler_params=pltpu.CompilerParams(vmem_limit_bytes=VMEM_LIMIT),
        cost_estimate=pl.CostEstimate(
            flops=2 * groups * z.pairs * z.local_ab * z.k * count,
            bytes_accessed=2 * z.local_ab * z.uc * LANES * count,
            transcendentals=0,
        ),
        name="ladder_piece",
    )(table, gathered, swapped, total, *[by_lines(x) for x in borrowed], *ints)


def swap_cores(x):
    return lax.ppermute(x, "col", [(i, i ^ 1) for i in range(lax.axis_size("col"))])


def over_row(x):
    return lax.ppermute(x, "row", [(0, 1), (1, 0)])


def over_chip(x):
    return lax.ppermute(x, "col", [(i, i ^ 2) for i in range(4)])


def pick(x, at, axis):
    return lax.dynamic_index_in_dim(x, at, axis, keepdims=False)


def reduce_plane(z, total):
    row, chip = lax.axis_index("row"), lax.axis_index("col") // 2

    def halve(x, at, axis, send):
        return pick(x, at, axis) + send(pick(x, 1 - at, axis))

    wide = z.local_ab // 2
    kept, given = total.reshape(2, 2, 2, z.half, z.local_ab)
    rest = kept + swap_cores(given)
    left, right = rest[..., :wide], rest[..., wide:]
    left = halve(left, row, 0, over_row)
    right = halve(right, chip, 1, over_chip)
    left = halve(left, chip, 0, over_chip)
    right = halve(right, row, 0, over_row)
    return jnp.concatenate([left, right], -1)


def per_device(amps, integrals, mask_amps, mask_ints):
    z = Sizes(amps, integrals)
    table = make_plan(z, mask_amps, mask_ints)
    groups = lax.axis_size("pair")

    def gather(own):
        return lax.all_gather(own, "pair")

    def add(piece, gathered, total, borrowed=()):
        return ladder_piece(z, table, piece, gathered, integrals, total, borrowed)

    def rare(total):
        return add(RARE, gather(pack(z, table, amps, RARE)), total)

    def finish(count, piece, own, second, total, borrowed):
        if count:
            last = gather(own[:count])
        if second is not None:
            total = add(SECOND, second, total, borrowed)
        if count:
            last, total = lax.optimization_barrier((last, total))
            total = add(piece, last, total)
        return total

    total = jnp.zeros((groups * z.pairs, z.local_ab), jnp.float32)
    head = pack(z, table, amps, HEAD)
    if z.long:
        first = gather(head)
        lent = over_chip(lend_amps(z, table, amps, 0)), over_row(lend_amps(z, table, amps, 1))
        ints = [[lend_integrals(z, table, integrals, way, part) for way in range(2)] for part in range(2)]
        lent, ints = lax.optimization_barrier((lent, ints))
        own = pack(z, table, amps, SECOND, lent)
        lower = over_chip(ints[0][0]), over_row(ints[0][1])
        third = pack(z, table, amps, THIRD)
        first, own, lower, third, rest = lax.optimization_barrier((first, own, lower, third, ints[1]))
        second = gather(own)
        upper = over_chip(rest[0]), over_row(rest[1])
        second, upper, total = lax.optimization_barrier((second, upper, add(HEAD, first, total)))
        borrowed = lower[0], upper[0], lower[1], upper[1]
        total = lax.cond(table[LONG] == 1, rare, lambda t: t, total)
        ends = [functools.partial(finish, n, THIRD) for n in range(PIECE + 1)]
        total = lax.switch(table[LAST], ends, third, second, total, borrowed)
    else:
        ends = [functools.partial(finish, n, HEAD) for n in range(1, PIECE + 1)]
        total = lax.switch(table[LAST] - 1, ends, head, None, total, ())

    if lax.axis_size("row") == 2 and lax.axis_size("col") == 4:
        ladder = lax.optimization_barrier(reduce_plane(z, total))
    else:
        halves = total.reshape(2, groups, z.half, z.local_ab)
        halves = jnp.where(table[CORE] == 0, halves, halves[::-1])
        total = jnp.swapaxes(halves, 0, 1).reshape(groups * z.pairs, z.local_ab)
        ladder = lax.psum_scatter(total, ("row", "col"), scatter_dimension=0, tiled=True)
    out_pairs = ladder.shape[0]
    local_a = WIN // groups
    grid = ladder.reshape(out_pairs, local_a, groups, local_a)
    received = lax.all_to_all(grid, "pair", split_axis=2, concat_axis=2, tiled=True)
    swapped = jnp.transpose(received, (0, 3, 2, 1)).reshape(out_pairs, local_a * WIN)
    return (0.5 * (ladder - swapped)).astype(jnp.bfloat16)


def solution(mesh):
    return jax.shard_map(
        per_device,
        mesh=mesh,
        in_specs=(P("pair", "row", "col"), P("pair", "row", "col"), P(), P()),
        out_specs=P(("row", "col"), "pair"),
        check_vma=False,
    )
```

```python
import functools

import jax
import jax.numpy as jnp
from jax import lax
from jax.experimental import pallas as pl
from jax.experimental.pallas import tpu as pltpu
from jax.sharding import PartitionSpec as P

TILE = 64
WIN = 64
LANES = 128
AB_BLOCK = 512
PIECE = 4
VMEM_LIMIT = 50 * 1024 * 1024

LAST, LONG, CORE, LENT, UNITS = 0, 1, 2, 3, 8
HEAD, SECOND, THIRD, RARE = 0, 1, 2, 3


class Sizes:
    def __init__(self, amps, integrals):
        self.pairs, self.local_c, self.local_d = amps.shape
        self.local_ab = integrals.shape[0]
        self.uc = min(self.local_c, TILE)
        self.ud = min(self.local_d, TILE)
        self.nud = self.local_d // self.ud
        self.units = (self.local_c // self.uc) * self.nud
        self.half = self.pairs // 2
        self.rows = self.uc // 2
        self.k = self.rows * LANES
        self.most = 2 * self.units
        self.long = self.most > PIECE
        self.places = (4 if self.long else 1) * PIECE
        self.slot_mine = UNITS + self.units
        self.slot_other = self.slot_mine + self.places
        self.fetch = self.slot_other + self.places
        self.fetch_tile = self.fetch + self.places
        self.table = self.fetch_tile + self.places


def lending(counts, here, there):
    move = jnp.minimum((here - there) // 2, 2)
    richer = jnp.where(counts[0] >= counts[1], 0, 1)
    return [jnp.where((counts[c] > 0) & ((move == 2) | ((move == 1) & (richer == c))), 1, 0) for c in range(2)]


def plan_kernel(z, rows, cols, pos_ref, ma_ref, mi_ref, table_ref):
    row, col = pos_ref[0], pos_ref[1]
    core, chip = lax.rem(col, 2), col // 2

    def active(r, c, unit):
        ct = (r * z.local_c + (unit // z.nud) * z.uc) // TILE
        dt = (c * z.local_d + lax.rem(unit, z.nud) * z.ud) // TILE
        return jnp.where(ma_ref[ct, dt] * mi_ref[ct, dt] != 0, 1, 0)

    def count(r, c):
        return lax.fori_loop(0, z.units, lambda u, n: n + active(r, c, u), 0)

    table_ref[CORE] = core
    for i in range(z.units):
        table_ref[UNITS + i] = 0

    def fill(u, n):
        on = active(row, col, u)

        @pl.when(on == 1)
        def _():
            table_ref[UNITS + n] = u

        return n + on

    own = lax.fori_loop(0, z.units, fill, 0)
    zero = jnp.int32(0)
    if z.long:
        grid = [(r, x) for r in range(2) for x in range(2)]
        n = {g: [count(g[0], 2 * g[1] + c) for c in range(2)] for g in grid}
        all_n = {g: n[g][0] + n[g][1] for g in grid}
        lent_x = {(r, x): lending(n[r, x], all_n[r, x], all_n[r, 1 - x]) for r, x in grid}
        n = {g: [n[g][c] - lent_x[g][c] for c in range(2)] for g in grid}
        all_n = {(r, x): sum(n[r, x]) + sum(lent_x[r, 1 - x]) for r, x in grid}
        lent_y = {(r, x): lending(n[r, x], all_n[r, x], all_n[1 - r, x]) for r, x in grid}
        n = {g: [n[g][c] - lent_y[g][c] for c in range(2)] for g in grid}
        all_n = {(r, x): sum(n[r, x]) + sum(lent_x[r, 1 - x]) + sum(lent_y[1 - r, x]) for r, x in grid}
        slots = jnp.int32(1)
        for g in grid:
            slots = jnp.maximum(slots, all_n[g])

        def here(get):
            upper = jnp.where(chip == 0, get(0, 0), get(0, 1))
            return jnp.where(row == 0, upper, jnp.where(chip == 0, get(1, 0), get(1, 1)))

        kept = [here(lambda r, x: n[r, x][c]) for c in range(2)]
        gives = [here(lambda r, x: jnp.where(core == 0, v[r, x][0], v[r, x][1])) for v in (lent_x, lent_y)]
        got = [here(lambda r, x: lent_x[r, 1 - x][c]) for c in range(2)]
        got += [here(lambda r, x: lent_y[1 - r, x][c]) for c in range(2)]
        is_long = slots > 3 * PIECE
        last_len = jnp.maximum(slots - jnp.where(is_long, 3, 2) * PIECE, 0)
    else:

        def most(g, n):
            r, x = g // (cols // 2), lax.rem(g, cols // 2)
            return jnp.maximum(n, count(r, 2 * x) + count(r, 2 * x + 1))

        slots = lax.fori_loop(0, rows * (cols // 2), most, 1)
        other = count(row, col + 1 - 2 * core)
        kept = [jnp.where(core == 0, own, other), jnp.where(core == 0, other, own)]
        gives, got = [zero, zero], [zero] * 4
        is_long, last_len = slots > PIECE, slots
    table_ref[LAST] = last_len
    table_ref[LONG] = jnp.where(is_long, 1, 0)
    for d in range(2):
        at = own - 1 - (gives[0] if d else 0)
        table_ref[LENT + d] = jnp.where(gives[d] == 1, table_ref[UNITS + jnp.clip(at, 0, z.units - 1)], -1)

    first, second = kept
    extra = jnp.abs(first - second)
    richer = jnp.where(first >= second, 0, 1)
    for at in range(z.places):
        piece, j = divmod(at, PIECE)
        borrowed = jnp.bool_(False)
        s = zero + at
        if piece == SECOND:
            borrowed = got[j] == 1
            s = s - sum(got[:j], zero)
        elif piece == THIRD:
            s = s - sum(got, zero) + jnp.where(is_long, PIECE, 0)
        elif piece == RARE:
            s = s - sum(got, zero) - PIECE
        live = jnp.logical_not(borrowed) & (s < first + second)
        if piece == RARE:
            live &= is_long
        k = s - extra
        owner = jnp.where(s < extra, richer, lax.rem(jnp.maximum(k, 0), 2))
        index = jnp.where(s < extra, s, k // 2 + jnp.where(owner == richer, extra, 0))
        unit = table_ref[UNITS + jnp.clip(index, 0, z.units - 1)]
        mine = jnp.where(live & (owner == core), unit, -1)
        theirs = live & (owner != core)
        if piece == SECOND:
            mine = jnp.where(borrowed & (core == j % 2), z.units + j // 2, mine)
            theirs |= borrowed & (core != j % 2)
        table_ref[z.slot_mine + at] = mine
        table_ref[z.slot_other + at] = jnp.where(theirs, 1, 0)
    for start in range(0, z.places, PIECE):
        units = [table_ref[z.slot_mine + start + j] for j in range(PIECE)]
        for place, limit in ((z.fetch, z.units + 2), (z.fetch_tile, z.units)):
            used = [(u >= 0) & (u < limit) for u in units]
            last = zero
            for j in reversed(range(PIECE)):
                last = jnp.where(used[j], j, last)
            for j in range(PIECE):
                last = jnp.where(used[j], j, last)
                if place == z.fetch:
                    table_ref[place + start + j] = last
                else:
                    unit = table_ref[z.slot_mine + start + last]
                    unit = jnp.where((unit >= 0) & (unit < limit), unit, 0)
                    table_ref[place + start + j] = unit // z.nud


def make_plan(z, mask_amps, mask_ints):
    rows, cols = lax.axis_size("row"), lax.axis_size("col")
    pos = jnp.stack([lax.axis_index("row"), lax.axis_index("col")]).astype(jnp.int32)
    smem = pl.BlockSpec(memory_space=pltpu.SMEM)
    return pl.pallas_call(
        functools.partial(plan_kernel, z, rows, cols),
        out_shape=jax.ShapeDtypeStruct((z.table,), jnp.int32),
        in_specs=[smem] * 3,
        out_specs=smem,
        name="plan",
    )(pos, mask_amps, mask_ints)


def squeeze_tile(second, x, y):
    low = lax.broadcasted_iota(jnp.int32, x.shape, 2) < TILE
    if second:
        return jnp.where(low, jnp.concatenate([x[..., TILE:], x[..., :TILE]], -1), y)
    return jnp.where(low, x, jnp.concatenate([y[..., TILE:], y[..., :TILE]], -1))


def pack_tile(z, unit, on, a_ref, o_ref):
    for second in range(z.nud):

        @pl.when(on & (lax.rem(unit, z.nud) == second))
        def _(second=second):
            v = squeeze_tile(second, a_ref[:, : z.rows, :], a_ref[:, z.rows :, :])
            o_ref[0] = v.reshape(z.half, z.k)


def pack_slots(z, table, amps, start, count, kept, borrowed=(), received=None):
    def unit_of(t, i):
        return t[z.slot_mine + start + i]

    def other(t, i):
        return t[z.slot_other + start + i]

    def half(t):
        return t[CORE] if kept else 1 - t[CORE]

    def tile(t, i):
        unit = unit_of(t, i)
        return jnp.where((unit >= 0) & (unit < z.units), unit, 0) // z.nud

    def body(t, a_ref, *refs):
        o_ref = refs[-1]
        i = pl.program_id(0)
        unit = unit_of(t, i)
        pack_tile(z, unit, (unit >= 0) & (unit < z.units), a_ref, o_ref)
        for d in range(len(borrowed)):

            @pl.when(unit == z.units + d)
            def _(d=d):
                o_ref[0] = refs[d][0]

        if kept:

            @pl.when(other(t, i) == 1)
            def _():
                o_ref[0] = refs[-2][0]

    in_specs = [pl.BlockSpec((z.half, z.uc, LANES), lambda i, t: (half(t), tile(t, i), 0))]
    in_specs += [pl.BlockSpec((1, z.half, z.k), lambda i, t: (half(t), 0, 0))] * len(borrowed)
    args = [amps, *borrowed]
    if kept:
        in_specs.append(pl.BlockSpec((1, z.half, z.k), lambda i, t: (jnp.where(other(t, i) == 1, i, 0), 0, 0)))
        args.append(received)
    return pl.pallas_call(
        body,
        grid_spec=pltpu.PrefetchScalarGridSpec(
            num_scalar_prefetch=1,
            grid=(count,),
            in_specs=in_specs,
            out_specs=pl.BlockSpec((1, z.half, z.k), lambda i, t: (i, 0, 0)),
        ),
        out_shape=jax.ShapeDtypeStruct((count, z.half, z.k), jnp.bfloat16),
        compiler_params=pltpu.CompilerParams(vmem_limit_bytes=VMEM_LIMIT),
        cost_estimate=pl.CostEstimate(flops=0, bytes_accessed=4 * count * z.half * z.k * 2, transcendentals=0),
        name="pack_kept" if kept else "pack_given",
    )(table, *args)


def lend_amps(z, table, amps, way):
    def body(t, a_ref, o_ref):
        unit = t[LENT + way]
        pack_tile(z, unit, unit >= 0, a_ref, o_ref)

    return pl.pallas_call(
        body,
        grid_spec=pltpu.PrefetchScalarGridSpec(
            num_scalar_prefetch=1,
            grid=(2,),
            in_specs=[
                pl.BlockSpec((z.half, z.uc, LANES), lambda h, t: (h, jnp.maximum(t[LENT + way], 0) // z.nud, 0))
            ],
            out_specs=pl.BlockSpec((1, z.half, z.k), lambda h, t: (h, 0, 0)),
        ),
        out_shape=jax.ShapeDtypeStruct((2, z.half, z.k), jnp.bfloat16),
        compiler_params=pltpu.CompilerParams(vmem_limit_bytes=VMEM_LIMIT),
        name="lend_amps",
    )(table, amps)


def lend_integrals(z, table, integrals, way, part):
    ab = AB_BLOCK // 2
    steps = z.local_ab // 2 // ab

    def body(t, x_ref, y_ref, o_ref):
        unit = t[LENT + way]
        for second in range(z.nud):

            @pl.when((unit >= 0) & (lax.rem(unit, z.nud) == second))
            def _(second=second):
                def relay(i):
                    at = pl.ds(i * 32, 32)
                    o_ref[at] = squeeze_tile(second, x_ref[at], y_ref[at])

                each(ab // 32, relay)

    def imap(offset):
        return lambda j, t: (part * steps + j, jnp.maximum(t[LENT + way], 0) // z.nud * 2 + offset, 0)

    return pl.pallas_call(
        body,
        grid_spec=pltpu.PrefetchScalarGridSpec(
            num_scalar_prefetch=1,
            grid=(steps,),
            in_specs=[pl.BlockSpec((ab, z.rows, LANES), imap(0)), pl.BlockSpec((ab, z.rows, LANES), imap(1))],
            out_specs=pl.BlockSpec((ab, z.rows, LANES), lambda j, t: (j, 0, 0)),
        ),
        out_shape=jax.ShapeDtypeStruct((z.local_ab // 2, z.rows, LANES), jnp.bfloat16),
        compiler_params=pltpu.CompilerParams(vmem_limit_bytes=VMEM_LIMIT),
        name="lend_integrals",
    )(table, integrals, integrals)


def pack(z, table, amps, piece, borrowed=()):
    start = piece * PIECE
    given = swap_cores(pack_slots(z, table, amps, start, PIECE, False, borrowed))
    return pack_slots(z, table, amps, start, PIECE, True, borrowed, given)


def each(count, body):
    def step(i, carry):
        body(i)
        return carry

    lax.fori_loop(0, count, step, 0)


def ladder_piece(z, table, piece, gathered, integrals, total, borrowed=()):
    groups, count = gathered.shape[:2]
    swapped = swap_cores(gathered)
    ab = min(AB_BLOCK // 2 if borrowed else AB_BLOCK, z.local_ab)
    parts = z.local_ab // ab
    few, many, deep = 64, 256, min(z.k, 1024)
    per_unit = z.uc // z.rows
    split = z.rows % 16 == 0
    m = groups * z.half

    def by_lines(x):
        return x.reshape(-1, few, *x.shape[1:])

    def unit_of(t, s):
        return t[z.slot_mine + piece * PIECE + s]

    def tile(t, s):
        return t[z.fetch_tile + piece * PIECE + s]

    def body(t, g_ref, w_ref, prev_ref, *rest):
        lent_refs, rest = rest[: len(borrowed)], rest[len(borrowed) :]
        if split:
            x_ref, y_ref, out_ref, b_ref = rest
        else:
            x_ref, out_ref, b_ref = rest
        s = pl.program_id(1)
        unit = unit_of(t, s)

        @pl.when(s == 0)
        def _():
            out_ref[...] = prev_ref[...]

        for second in range(z.nud):

            @pl.when((unit >= 0) & (unit < z.units) & (lax.rem(unit, z.nud) == second))
            def _(second=second):
                def relay(i):
                    if split:
                        x, y = x_ref[i], y_ref[i]
                    else:
                        x, y = x_ref[i, :, : z.rows], x_ref[i, :, z.rows :]
                    b_ref[i] = squeeze_tile(second, x, y).reshape(few, z.k)

                each(ab // few, relay)

        for d in range(len(borrowed)):
            upper = pl.program_id(0) >= parts // 2

            @pl.when((unit == z.units + d // 2) & (upper == (d % 2 == 1)))
            def _(d=d):
                def relay(i):
                    b_ref[i] = lent_refs[d][i].reshape(few, z.k)

                each(ab // few, relay)

        @pl.when(unit >= 0)
        def _():
            def product(i):
                n, k = i // (z.k // deep), lax.rem(i, z.k // deep)
                at = pl.ds(pl.multiple_of(n * many, many), many)
                cols = pl.ds(pl.multiple_of(k * deep, deep), deep)
                b = b_ref[pl.ds(n * (many // few), many // few), :, cols].reshape(many, deep)
                for h, a_ref in enumerate((g_ref, w_ref)):
                    out_ref[h * m : (h + 1) * m, at] += lax.dot_general(
                        a_ref[:, 0, :, cols].reshape(m, deep),
                        b,
                        (((1,), (1,)), ((), ())),
                        preferred_element_type=jnp.float32,
                    )

            each((ab // many) * (z.k // deep), product)

    def imap(offset):
        def index(j, s, t):
            return (j, 0, tile(t, s) * per_unit + offset, 0)

        return index

    piece_spec = pl.BlockSpec((groups, 1, z.half, z.k), lambda j, s, t: (0, t[z.fetch + piece * PIECE + s], 0, 0))
    out_spec = pl.BlockSpec((groups * z.pairs, ab), lambda j, s, t: (0, j))
    if split:
        ints_specs = [pl.BlockSpec((ab // few, few, z.rows, LANES), imap(offset)) for offset in range(2)]
        ints = [by_lines(integrals)] * 2
    else:
        ints_specs = [pl.BlockSpec((ab // few, few, z.uc, LANES), lambda j, s, t: (j, 0, tile(t, s), 0))]
        ints = [by_lines(integrals)]
    low_spec = pl.BlockSpec((ab // few, few, z.rows, LANES), lambda j, s, t: (jnp.minimum(j, parts // 2 - 1), 0, 0, 0))
    high_spec = pl.BlockSpec((ab // few, few, z.rows, LANES), lambda j, s, t: (jnp.maximum(j - parts // 2, 0), 0, 0, 0))
    lent_specs = [low_spec, high_spec] * (len(borrowed) // 2)
    return pl.pallas_call(
        body,
        grid_spec=pltpu.PrefetchScalarGridSpec(
            num_scalar_prefetch=1,
            grid=(z.local_ab // ab, count),
            in_specs=[piece_spec, piece_spec, out_spec] + lent_specs + ints_specs,
            out_specs=out_spec,
            scratch_shapes=[pltpu.VMEM((ab // few, few, z.k), jnp.bfloat16)],
        ),
        out_shape=jax.ShapeDtypeStruct((groups * z.pairs, z.local_ab), jnp.float32),
        input_output_aliases={3: 0},
        compiler_params=pltpu.CompilerParams(vmem_limit_bytes=VMEM_LIMIT),
        cost_estimate=pl.CostEstimate(
            flops=2 * groups * z.pairs * z.local_ab * z.k * count,
            bytes_accessed=2 * z.local_ab * z.uc * LANES * count,
            transcendentals=0,
        ),
        name="ladder_piece",
    )(table, gathered, swapped, total, *[by_lines(x) for x in borrowed], *ints)


def swap_cores(x):
    return lax.ppermute(x, "col", [(i, i ^ 1) for i in range(lax.axis_size("col"))])


def over_row(x):
    return lax.ppermute(x, "row", [(0, 1), (1, 0)])


def over_chip(x):
    return lax.ppermute(x, "col", [(i, i ^ 2) for i in range(4)])


def pick(x, at, axis):
    return lax.dynamic_index_in_dim(x, at, axis, keepdims=False)


def reduce_plane(z, total):
    row, chip = lax.axis_index("row"), lax.axis_index("col") // 2

    def halve(x, at, axis, send):
        return pick(x, at, axis) + send(pick(x, 1 - at, axis))

    wide = z.local_ab // 2
    kept, given = total.reshape(2, 2, 2, z.half, z.local_ab)
    rest = kept + swap_cores(given)
    left, right = rest[..., :wide], rest[..., wide:]
    left = halve(left, row, 0, over_row)
    right = halve(right, chip, 1, over_chip)
    left = halve(left, chip, 0, over_chip)
    right = halve(right, row, 0, over_row)
    return jnp.concatenate([left, right], -1)


def per_device(amps, integrals, mask_amps, mask_ints):
    z = Sizes(amps, integrals)
    table = make_plan(z, mask_amps, mask_ints)
    groups = lax.axis_size("pair")

    def gather(own):
        return lax.all_gather(own, "pair")

    def add(piece, gathered, total, borrowed=()):
        return ladder_piece(z, table, piece, gathered, integrals, total, borrowed)

    def rare(total):
        return add(RARE, gather(pack(z, table, amps, RARE)), total)

    def finish(count, piece, own, second, total, borrowed):
        if count:
            last = gather(own[:count])
        if second is not None:
            total = add(SECOND, second, total, borrowed)
        if count:
            last, total = lax.optimization_barrier((last, total))
            total = add(piece, last, total)
        return total

    total = jnp.zeros((groups * z.pairs, z.local_ab), jnp.float32)
    head = pack(z, table, amps, HEAD)
    if z.long:
        first = gather(head)
        lent = over_chip(lend_amps(z, table, amps, 0)), over_row(lend_amps(z, table, amps, 1))
        ints = [[lend_integrals(z, table, integrals, way, part) for way in range(2)] for part in range(2)]
        lent, ints = lax.optimization_barrier((lent, ints))
        own = pack(z, table, amps, SECOND, lent)
        lower = over_chip(ints[0][0]), over_row(ints[0][1])
        third = pack(z, table, amps, THIRD)
        first, own, lower, third, rest = lax.optimization_barrier((first, own, lower, third, ints[1]))
        second = gather(own)
        upper = over_chip(rest[0]), over_row(rest[1])
        second, upper, total = lax.optimization_barrier((second, upper, add(HEAD, first, total)))
        borrowed = lower[0], upper[0], lower[1], upper[1]
        total = lax.cond(table[LONG] == 1, rare, lambda t: t, total)
        ends = [functools.partial(finish, n, THIRD) for n in range(PIECE + 1)]
        total = lax.switch(table[LAST], ends, third, second, total, borrowed)
    else:
        ends = [functools.partial(finish, n, HEAD) for n in range(1, PIECE + 1)]
        total = lax.switch(table[LAST] - 1, ends, head, None, total, ())

    if lax.axis_size("row") == 2 and lax.axis_size("col") == 4:
        ladder = lax.optimization_barrier(reduce_plane(z, total))
    else:
        halves = total.reshape(2, groups, z.half, z.local_ab)
        halves = jnp.where(table[CORE] == 0, halves, halves[::-1])
        total = jnp.swapaxes(halves, 0, 1).reshape(groups * z.pairs, z.local_ab)
        ladder = lax.psum_scatter(total, ("row", "col"), scatter_dimension=0, tiled=True)
    out_pairs = ladder.shape[0]
    local_a = WIN // groups
    grid = ladder.reshape(out_pairs, local_a, groups, local_a)
    received = lax.all_to_all(grid, "pair", split_axis=2, concat_axis=2, tiled=True)
    swapped = jnp.transpose(received, (0, 3, 2, 1)).reshape(out_pairs, local_a * WIN)
    return (0.5 * (ladder - swapped)).astype(jnp.bfloat16)


def solution(mesh):
    return jax.shard_map(
        per_device,
        mesh=mesh,
        in_specs=(P("pair", "row", "col"), P("pair", "row", "col"), P(), P()),
        out_specs=P(("row", "col"), "pair"),
        check_vma=False,
    )
```

```python
import functools

import jax
import jax.numpy as jnp
from jax import lax
from jax.experimental import pallas as pl
from jax.experimental.pallas import tpu as pltpu
from jax.sharding import PartitionSpec as P

TILE = 64
WIN = 64
LANES = 128
AB_BLOCK = 512
PIECE = 4
VMEM_LIMIT = 56 * 1024 * 1024

LAST, LONG, CORE, LENT, UNITS = 0, 1, 2, 3, 8
HEAD, SECOND, THIRD, RARE = 0, 1, 2, 3


class Sizes:
    def __init__(self, amps, integrals):
        self.pairs, self.local_c, self.local_d = amps.shape
        self.local_ab = integrals.shape[0]
        self.uc = min(self.local_c, TILE)
        self.ud = min(self.local_d, TILE)
        self.nud = self.local_d // self.ud
        self.units = (self.local_c // self.uc) * self.nud
        self.half = self.pairs // 2
        self.rows = self.uc // 2
        self.k = self.rows * LANES
        self.most = 2 * self.units
        self.long = self.most > PIECE
        self.places = (4 if self.long else 1) * PIECE
        self.slot_mine = UNITS + self.units
        self.slot_other = self.slot_mine + self.places
        self.fetch = self.slot_other + self.places
        self.fetch_tile = self.fetch + self.places
        self.table = self.fetch_tile + self.places


def lending(counts, here, there):
    move = jnp.minimum((here - there) // 2, 2)
    richer = jnp.where(counts[0] >= counts[1], 0, 1)
    return [jnp.where((counts[c] > 0) & ((move == 2) | ((move == 1) & (richer == c))), 1, 0) for c in range(2)]


def plan_kernel(z, rows, cols, pos_ref, ma_ref, mi_ref, table_ref):
    row, col = pos_ref[0], pos_ref[1]
    core, chip = lax.rem(col, 2), col // 2

    def active(r, c, unit):
        ct = (r * z.local_c + (unit // z.nud) * z.uc) // TILE
        dt = (c * z.local_d + lax.rem(unit, z.nud) * z.ud) // TILE
        return jnp.where(ma_ref[ct, dt] * mi_ref[ct, dt] != 0, 1, 0)

    def count(r, c):
        return lax.fori_loop(0, z.units, lambda u, n: n + active(r, c, u), 0)

    table_ref[CORE] = core
    for i in range(z.units):
        table_ref[UNITS + i] = 0

    def fill(u, n):
        on = active(row, col, u)

        @pl.when(on == 1)
        def _():
            table_ref[UNITS + n] = u

        return n + on

    own = lax.fori_loop(0, z.units, fill, 0)
    zero = jnp.int32(0)
    if z.long:
        grid = [(r, x) for r in range(2) for x in range(2)]
        n = {g: [count(g[0], 2 * g[1] + c) for c in range(2)] for g in grid}
        all_n = {g: n[g][0] + n[g][1] for g in grid}
        lent_x = {(r, x): lending(n[r, x], all_n[r, x], all_n[r, 1 - x]) for r, x in grid}
        n = {g: [n[g][c] - lent_x[g][c] for c in range(2)] for g in grid}
        all_n = {(r, x): sum(n[r, x]) + sum(lent_x[r, 1 - x]) for r, x in grid}
        lent_y = {(r, x): lending(n[r, x], all_n[r, x], all_n[1 - r, x]) for r, x in grid}
        n = {g: [n[g][c] - lent_y[g][c] for c in range(2)] for g in grid}
        all_n = {(r, x): sum(n[r, x]) + sum(lent_x[r, 1 - x]) + sum(lent_y[1 - r, x]) for r, x in grid}
        slots = jnp.int32(1)
        for g in grid:
            slots = jnp.maximum(slots, all_n[g])

        def here(get):
            upper = jnp.where(chip == 0, get(0, 0), get(0, 1))
            return jnp.where(row == 0, upper, jnp.where(chip == 0, get(1, 0), get(1, 1)))

        kept = [here(lambda r, x: n[r, x][c]) for c in range(2)]
        gives = [here(lambda r, x: jnp.where(core == 0, v[r, x][0], v[r, x][1])) for v in (lent_x, lent_y)]
        got = [here(lambda r, x: lent_x[r, 1 - x][c]) for c in range(2)]
        got += [here(lambda r, x: lent_y[1 - r, x][c]) for c in range(2)]
        is_long = slots > 3 * PIECE
        last_len = jnp.maximum(slots - jnp.where(is_long, 3, 2) * PIECE, 0)
    else:

        def most(g, n):
            r, x = g // (cols // 2), lax.rem(g, cols // 2)
            return jnp.maximum(n, count(r, 2 * x) + count(r, 2 * x + 1))

        slots = lax.fori_loop(0, rows * (cols // 2), most, 1)
        other = count(row, col + 1 - 2 * core)
        kept = [jnp.where(core == 0, own, other), jnp.where(core == 0, other, own)]
        gives, got = [zero, zero], [zero] * 4
        is_long, last_len = slots > PIECE, slots
    table_ref[LAST] = last_len
    table_ref[LONG] = jnp.where(is_long, 1, 0)
    for d in range(2):
        at = own - 1 - (gives[0] if d else 0)
        table_ref[LENT + d] = jnp.where(gives[d] == 1, table_ref[UNITS + jnp.clip(at, 0, z.units - 1)], -1)

    first, second = kept
    extra = jnp.abs(first - second)
    richer = jnp.where(first >= second, 0, 1)
    begins = jnp.where(got[0] + got[2] > got[1] + got[3], 1, 0)
    begins = lax.rem(begins + jnp.maximum(PIECE - extra, 0), 2)
    for at in range(z.places):
        piece, j = divmod(at, PIECE)
        borrowed = jnp.bool_(False)
        s = zero + at
        if piece == SECOND:
            borrowed = got[j] == 1
            s = s - sum(got[:j], zero)
        elif piece == THIRD:
            s = s - sum(got, zero) + jnp.where(is_long, PIECE, 0)
        elif piece == RARE:
            s = s - sum(got, zero) - PIECE
        live = jnp.logical_not(borrowed) & (s < first + second)
        if piece == RARE:
            live &= is_long
        k = s - extra
        owner = jnp.where(s < extra, richer, lax.rem(jnp.maximum(k, 0) + begins, 2))
        index = jnp.where(s < extra, s, k // 2 + jnp.where(owner == richer, extra, 0))
        unit = table_ref[UNITS + jnp.clip(index, 0, z.units - 1)]
        mine = jnp.where(live & (owner == core), unit, -1)
        theirs = live & (owner != core)
        if piece == SECOND:
            mine = jnp.where(borrowed & (core == j % 2), z.units + j // 2, mine)
            theirs |= borrowed & (core != j % 2)
        table_ref[z.slot_mine + at] = mine
        table_ref[z.slot_other + at] = jnp.where(theirs, 1, 0)
    for start in range(0, z.places, PIECE):
        units = [table_ref[z.slot_mine + start + j] for j in range(PIECE)]
        for place, limit in ((z.fetch, z.units + 2), (z.fetch_tile, z.units)):
            used = [(u >= 0) & (u < limit) for u in units]
            last = zero
            for j in reversed(range(PIECE)):
                last = jnp.where(used[j], j, last)
            for j in range(PIECE):
                last = jnp.where(used[j], j, last)
                if place == z.fetch:
                    table_ref[place + start + j] = last
                else:
                    unit = table_ref[z.slot_mine + start + last]
                    unit = jnp.where((unit >= 0) & (unit < limit), unit, 0)
                    table_ref[place + start + j] = unit // z.nud


def make_plan(z, mask_amps, mask_ints):
    rows, cols = lax.axis_size("row"), lax.axis_size("col")
    pos = jnp.stack([lax.axis_index("row"), lax.axis_index("col")]).astype(jnp.int32)
    smem = pl.BlockSpec(memory_space=pltpu.SMEM)
    return pl.pallas_call(
        functools.partial(plan_kernel, z, rows, cols),
        out_shape=jax.ShapeDtypeStruct((z.table,), jnp.int32),
        in_specs=[smem] * 3,
        out_specs=smem,
        name="plan",
    )(pos, mask_amps, mask_ints)


def squeeze_tile(second, x, y):
    low = lax.broadcasted_iota(jnp.int32, x.shape, 2) < TILE
    if second:
        return jnp.where(low, jnp.concatenate([x[..., TILE:], x[..., :TILE]], -1), y)
    return jnp.where(low, x, jnp.concatenate([y[..., TILE:], y[..., :TILE]], -1))


def pack_tile(z, unit, on, a_ref, o_ref):
    for second in range(z.nud):

        @pl.when(on & (lax.rem(unit, z.nud) == second))
        def _(second=second):
            v = squeeze_tile(second, a_ref[:, : z.rows, :], a_ref[:, z.rows :, :])
            o_ref[0] = v.reshape(z.half, z.k)


def pack_slots(z, table, amps, start, count, kept, borrowed=(), received=None):
    def unit_of(t, i):
        return t[z.slot_mine + start + i]

    def other(t, i):
        return t[z.slot_other + start + i]

    def half(t):
        return t[CORE] if kept else 1 - t[CORE]

    def tile(t, i):
        unit = unit_of(t, i)
        return jnp.where((unit >= 0) & (unit < z.units), unit, 0) // z.nud

    def body(t, a_ref, *refs):
        o_ref = refs[-1]
        i = pl.program_id(0)
        unit = unit_of(t, i)
        pack_tile(z, unit, (unit >= 0) & (unit < z.units), a_ref, o_ref)
        for d in range(len(borrowed)):

            @pl.when(unit == z.units + d)
            def _(d=d):
                o_ref[0] = refs[d][0]

        if kept:

            @pl.when(other(t, i) == 1)
            def _():
                o_ref[0] = refs[-2][0]

    in_specs = [pl.BlockSpec((z.half, z.uc, LANES), lambda i, t: (half(t), tile(t, i), 0))]
    in_specs += [pl.BlockSpec((1, z.half, z.k), lambda i, t: (half(t), 0, 0))] * len(borrowed)
    args = [amps, *borrowed]
    if kept:
        in_specs.append(pl.BlockSpec((1, z.half, z.k), lambda i, t: (jnp.where(other(t, i) == 1, i, 0), 0, 0)))
        args.append(received)
    return pl.pallas_call(
        body,
        grid_spec=pltpu.PrefetchScalarGridSpec(
            num_scalar_prefetch=1,
            grid=(count,),
            in_specs=in_specs,
            out_specs=pl.BlockSpec((1, z.half, z.k), lambda i, t: (i, 0, 0)),
        ),
        out_shape=jax.ShapeDtypeStruct((count, z.half, z.k), jnp.bfloat16),
        compiler_params=pltpu.CompilerParams(vmem_limit_bytes=VMEM_LIMIT),
        cost_estimate=pl.CostEstimate(flops=0, bytes_accessed=4 * count * z.half * z.k * 2, transcendentals=0),
        name="pack_kept" if kept else "pack_given",
    )(table, *args)


def lend_amps(z, table, amps, way):
    def body(t, a_ref, o_ref):
        unit = t[LENT + way]
        pack_tile(z, unit, unit >= 0, a_ref, o_ref)

    return pl.pallas_call(
        body,
        grid_spec=pltpu.PrefetchScalarGridSpec(
            num_scalar_prefetch=1,
            grid=(2,),
            in_specs=[
                pl.BlockSpec((z.half, z.uc, LANES), lambda h, t: (h, jnp.maximum(t[LENT + way], 0) // z.nud, 0))
            ],
            out_specs=pl.BlockSpec((1, z.half, z.k), lambda h, t: (h, 0, 0)),
        ),
        out_shape=jax.ShapeDtypeStruct((2, z.half, z.k), jnp.bfloat16),
        compiler_params=pltpu.CompilerParams(vmem_limit_bytes=VMEM_LIMIT),
        name="lend_amps",
    )(table, amps)


def lend_integrals(z, table, integrals, way, part):
    ab = AB_BLOCK // 2
    steps = z.local_ab // 2 // ab

    def body(t, x_ref, y_ref, o_ref):
        unit = t[LENT + way]
        for second in range(z.nud):

            @pl.when((unit >= 0) & (lax.rem(unit, z.nud) == second))
            def _(second=second):
                def relay(i):
                    at = pl.ds(i * 32, 32)
                    o_ref[at] = squeeze_tile(second, x_ref[at], y_ref[at])

                each(ab // 32, relay)

    def imap(offset):
        return lambda j, t: (part * steps + j, jnp.maximum(t[LENT + way], 0) // z.nud * 2 + offset, 0)

    return pl.pallas_call(
        body,
        grid_spec=pltpu.PrefetchScalarGridSpec(
            num_scalar_prefetch=1,
            grid=(steps,),
            in_specs=[pl.BlockSpec((ab, z.rows, LANES), imap(0)), pl.BlockSpec((ab, z.rows, LANES), imap(1))],
            out_specs=pl.BlockSpec((ab, z.rows, LANES), lambda j, t: (j, 0, 0)),
        ),
        out_shape=jax.ShapeDtypeStruct((z.local_ab // 2, z.rows, LANES), jnp.bfloat16),
        compiler_params=pltpu.CompilerParams(vmem_limit_bytes=VMEM_LIMIT),
        name="lend_integrals",
    )(table, integrals, integrals)


def pack(z, table, amps, piece, borrowed=()):
    start = piece * PIECE
    given = swap_cores(pack_slots(z, table, amps, start, PIECE, False, borrowed))
    return pack_slots(z, table, amps, start, PIECE, True, borrowed, given)


def each(count, body):
    def step(i, carry):
        body(i)
        return carry

    lax.fori_loop(0, count, step, 0)


def ladder_piece(z, table, piece, gathered, integrals, total, borrowed=()):
    groups, count = gathered.shape[:2]
    swapped = swap_cores(gathered)
    ab = min(AB_BLOCK, z.local_ab)
    parts = z.local_ab // ab
    few, many, deep = 64, 256, min(z.k, 1024)
    per_unit = z.uc // z.rows
    split = z.rows % 16 == 0
    m = groups * z.half

    def by_lines(x):
        return x.reshape(-1, few, *x.shape[1:])

    def unit_of(t, s):
        return t[z.slot_mine + piece * PIECE + s]

    def tile(t, s):
        return t[z.fetch_tile + piece * PIECE + s]

    def body(t, g_ref, w_ref, prev_ref, *rest):
        lent_refs, rest = rest[: len(borrowed)], rest[len(borrowed) :]
        if split:
            x_ref, y_ref, out_ref, b_ref = rest
        else:
            x_ref, out_ref, b_ref = rest
        s = pl.program_id(1)
        unit = unit_of(t, s)

        @pl.when(s == 0)
        def _():
            out_ref[...] = prev_ref[...]

        for second in range(z.nud):

            @pl.when((unit >= 0) & (unit < z.units) & (lax.rem(unit, z.nud) == second))
            def _(second=second):
                def relay(i):
                    if split:
                        x, y = x_ref[i], y_ref[i]
                    else:
                        x, y = x_ref[i, :, : z.rows], x_ref[i, :, z.rows :]
                    b_ref[i] = squeeze_tile(second, x, y).reshape(few, z.k)

                each(ab // few, relay)

        for d in range(len(borrowed)):
            upper = pl.program_id(0) >= parts // 2

            @pl.when((unit == z.units + d // 2) & (upper == (d % 2 == 1)))
            def _(d=d):
                def relay(i):
                    b_ref[i] = lent_refs[d][i].reshape(few, z.k)

                each(ab // few, relay)

        @pl.when(unit >= 0)
        def _():
            def product(i):
                n, k = i // (z.k // deep), lax.rem(i, z.k // deep)
                at = pl.ds(pl.multiple_of(n * many, many), many)
                cols = pl.ds(pl.multiple_of(k * deep, deep), deep)
                b = b_ref[pl.ds(n * (many // few), many // few), :, cols].reshape(many, deep)
                for h, a_ref in enumerate((g_ref, w_ref)):
                    out_ref[h * m : (h + 1) * m, at] += lax.dot_general(
                        a_ref[:, 0, :, cols].reshape(m, deep),
                        b,
                        (((1,), (1,)), ((), ())),
                        preferred_element_type=jnp.float32,
                    )

            each((ab // many) * (z.k // deep), product)

    def imap(offset):
        def index(j, s, t):
            return (j, 0, tile(t, s) * per_unit + offset, 0)

        return index

    piece_spec = pl.BlockSpec((groups, 1, z.half, z.k), lambda j, s, t: (0, t[z.fetch + piece * PIECE + s], 0, 0))
    out_spec = pl.BlockSpec((groups * z.pairs, ab), lambda j, s, t: (0, j))
    if split:
        ints_specs = [pl.BlockSpec((ab // few, few, z.rows, LANES), imap(offset)) for offset in range(2)]
        ints = [by_lines(integrals)] * 2
    else:
        ints_specs = [pl.BlockSpec((ab // few, few, z.uc, LANES), lambda j, s, t: (j, 0, tile(t, s), 0))]
        ints = [by_lines(integrals)]
    once = pl.Buffered(1)
    low_spec = pl.BlockSpec((ab // few, few, z.rows, LANES), lambda j, s, t: (jnp.minimum(j, parts // 2 - 1), 0, 0, 0), pipeline_mode=once)
    high_spec = pl.BlockSpec((ab // few, few, z.rows, LANES), lambda j, s, t: (jnp.maximum(j - parts // 2, 0), 0, 0, 0), pipeline_mode=once)
    lent_specs = [low_spec, high_spec] * (len(borrowed) // 2)
    return pl.pallas_call(
        body,
        grid_spec=pltpu.PrefetchScalarGridSpec(
            num_scalar_prefetch=1,
            grid=(z.local_ab // ab, count),
            in_specs=[piece_spec, piece_spec, out_spec] + lent_specs + ints_specs,
            out_specs=out_spec,
            scratch_shapes=[pltpu.VMEM((ab // few, few, z.k), jnp.bfloat16)],
        ),
        out_shape=jax.ShapeDtypeStruct((groups * z.pairs, z.local_ab), jnp.float32),
        input_output_aliases={3: 0},
        compiler_params=pltpu.CompilerParams(vmem_limit_bytes=VMEM_LIMIT),
        cost_estimate=pl.CostEstimate(
            flops=2 * groups * z.pairs * z.local_ab * z.k * count,
            bytes_accessed=2 * z.local_ab * z.uc * LANES * count,
            transcendentals=0,
        ),
        name="ladder_piece",
    )(table, gathered, swapped, total, *[by_lines(x) for x in borrowed], *ints)


def swap_cores(x):
    return lax.ppermute(x, "col", [(i, i ^ 1) for i in range(lax.axis_size("col"))])


def over_row(x):
    return lax.ppermute(x, "row", [(0, 1), (1, 0)])


def over_chip(x):
    return lax.ppermute(x, "col", [(i, i ^ 2) for i in range(4)])


def pick(x, at, axis):
    return lax.dynamic_index_in_dim(x, at, axis, keepdims=False)


def reduce_plane(z, total):
    row, chip = lax.axis_index("row"), lax.axis_index("col") // 2

    def halve(x, at, axis, send):
        return pick(x, at, axis) + send(pick(x, 1 - at, axis))

    wide = z.local_ab // 2
    kept, given = total.reshape(2, 2, 2, z.half, z.local_ab)
    rest = kept + swap_cores(given)
    left, right = rest[..., :wide], rest[..., wide:]
    left = halve(left, row, 0, over_row)
    right = halve(right, chip, 1, over_chip)
    left = halve(left, chip, 0, over_chip)
    right = halve(right, row, 0, over_row)
    return jnp.concatenate([left, right], -1)


def per_device(amps, integrals, mask_amps, mask_ints):
    z = Sizes(amps, integrals)
    table = make_plan(z, mask_amps, mask_ints)
    groups = lax.axis_size("pair")

    def gather(own):
        return lax.all_gather(own, "pair")

    def add(piece, gathered, total, borrowed=()):
        return ladder_piece(z, table, piece, gathered, integrals, total, borrowed)

    def rare(total):
        return add(RARE, gather(pack(z, table, amps, RARE)), total)

    def finish(count, piece, own, second, total, borrowed):
        if count:
            last = gather(own[:count])
        if second is not None:
            total = add(SECOND, second, total, borrowed)
        if count:
            last, total = lax.optimization_barrier((last, total))
            total = add(piece, last, total)
        return total

    total = jnp.zeros((groups * z.pairs, z.local_ab), jnp.float32)
    head = pack(z, table, amps, HEAD)
    if z.long:
        first = gather(head)
        lent = over_chip(lend_amps(z, table, amps, 0)), over_row(lend_amps(z, table, amps, 1))
        ints = [[lend_integrals(z, table, integrals, way, part) for way in range(2)] for part in range(2)]
        lent, ints = lax.optimization_barrier((lent, ints))
        own = pack(z, table, amps, SECOND, lent)
        lower = over_chip(ints[0][0]), over_row(ints[0][1])
        third = pack(z, table, amps, THIRD)
        first, own, lower, third, rest = lax.optimization_barrier((first, own, lower, third, ints[1]))
        second = gather(own)
        upper = over_chip(rest[0]), over_row(rest[1])
        second, upper, total = lax.optimization_barrier((second, upper, add(HEAD, first, total)))
        borrowed = lower[0], upper[0], lower[1], upper[1]
        total = lax.cond(table[LONG] == 1, rare, lambda t: t, total)
        ends = [functools.partial(finish, n, THIRD) for n in range(PIECE + 1)]
        total = lax.switch(table[LAST], ends, third, second, total, borrowed)
    else:
        ends = [functools.partial(finish, n, HEAD) for n in range(1, PIECE + 1)]
        total = lax.switch(table[LAST] - 1, ends, head, None, total, ())

    if lax.axis_size("row") == 2 and lax.axis_size("col") == 4:
        ladder = lax.optimization_barrier(reduce_plane(z, total))
    else:
        halves = total.reshape(2, groups, z.half, z.local_ab)
        halves = jnp.where(table[CORE] == 0, halves, halves[::-1])
        total = jnp.swapaxes(halves, 0, 1).reshape(groups * z.pairs, z.local_ab)
        ladder = lax.psum_scatter(total, ("row", "col"), scatter_dimension=0, tiled=True)
    out_pairs = ladder.shape[0]
    local_a = WIN // groups
    grid = ladder.reshape(out_pairs, local_a, groups, local_a)
    received = lax.all_to_all(grid, "pair", split_axis=2, concat_axis=2, tiled=True)
    swapped = jnp.transpose(received, (0, 3, 2, 1)).reshape(out_pairs, local_a * WIN)
    return (0.5 * (ladder - swapped)).astype(jnp.bfloat16)


def solution(mesh):
    return jax.shard_map(
        per_device,
        mesh=mesh,
        in_specs=(P("pair", "row", "col"), P("pair", "row", "col"), P(), P()),
        out_specs=P(("row", "col"), "pair"),
        check_vma=False,
    )
```
